128 devices in a mesh: gx: 16 (over y, x_hi, core), gy: 8 (over z, x_lo).
Axes of the slice: x: 4 (x_hi: 2, x_lo: 2; x = x_hi * 2 + x_lo), y: 4, z: 4, core: 2. Of those that a mesh axis runs over, the one named last changes fastest.
Arguments:
- obj: float32 [2, 4096, 8192], P(None, 'gy', 'gx'), may hold values from -6 to 6
- probe: float32 [2, 256, 256], replicated, may hold values from -6 to 6
- intensity: float32 [2048, 256, 256], P(('gx', 'gy')), may hold values from 0.1 to 4
- dest: int32 [2048, 1], P(('gx', 'gy')), may hold values from 0 to 15; in each aligned block of 16 rows (0 to 15, 16 to 31, ...) at most 2 rows name the same one
- offsets: int32 [2048, 2], P(('gx', 'gy')), may hold values from 0 to 511
Outputs:
- new_obj: float32 [2, 4096, 8192], P(None, 'gy', 'gx')
The draws below stay inside these ranges and needn't reach their ends.
Inputs may be any that keep to these rules, and one draw needn't show every extreme that they name: `dest`: in each aligned block of 16 rows (the frames of one device) no tile column is named by more than 2 rows.
All inputs are finite; a program needn't handle non-finite values.
Results may differ from the reference program's by a relative error of at most 0.006.
Values may be sent and summed in bfloat16 or wider, within the bound.
No kernel may reach another device: no remote copies, remote signals or barrier semaphores. Data moves between devices by JAX's collectives and lax.ppermute only.
A program may use at most 192 MiB of HBM per device.

```python
import math
import jax
import jax.numpy as jnp
import numpy as np
from jax import lax

P_SIZE = 256
TILE = 512
FRAMES_DEV = 16
CAP = 2
NR = 4096
NC = 8192
FRAMES = 2048
N_GX = 16
N_GY = 8


def place_ends(drawn, own_key, smallest, high):
    index_at = [jax.random.randint(jax.random.fold_in(own_key, axis), (), 0, length) for axis, length in enumerate(drawn.shape)]
    main_axis = drawn.shape.index(max(drawn.shape))
    beside = index_at[:main_axis] + [(index_at[main_axis] + 1) % drawn.shape[main_axis]] + index_at[main_axis + 1:]
    return drawn.at[tuple(index_at)].set(smallest).at[tuple(beside)].set(high)


def block_scale(rng, dims, cuts, low, high):
    factor_of, own = 1.0, jax.random.fold_in(rng, 6)
    for position, blocks in cuts:
        heights = jnp.exp(jax.random.uniform(jax.random.fold_in(own, position), (blocks,), jnp.float32, low / len(cuts), high / len(cuts)))
        factor_of = factor_of * jnp.repeat(heights, dims[position] // blocks).reshape([-1 if axis == position else 1 for axis in range(len(dims))])
    return factor_of


def deal_out(own_key, own, number, rows, count, top, most, lean):
    ranking = jax.random.permutation(own_key, count)
    crowded, usual = load_shares(count, rows * top, most, lean, True), load_shares(count, rows * top, most, lean, False)
    places = jnp.arange(count)

    def named(sizes, offset_by):
        used = int((sizes > 0).sum())
        fixed = max(1, used // 4)
        moved = fixed + (places - fixed + offset_by * (used - fixed)) % max(1, count - fixed)
        return jnp.zeros((count,), jnp.int32).at[ranking[jnp.where(places < fixed, places, moved)]].set(jnp.asarray(sizes, jnp.int32))

    sizes = jnp.where(number % 4 == 0, named(crowded, number // 4), named(usual, number - number // 4 - 1))
    mixed = jax.random.permutation(jax.random.fold_in(own, 3), count)
    donor, sink = mixed[0:count // 2 * 2:2], mixed[1:count // 2 * 2:2]
    slack = jnp.minimum(sizes[donor] - 1, most - sizes[sink]) // 2
    slack = jnp.where((donor == ranking[0]) | (sink == ranking[0]) | (sizes[sink] == 0), 0, jnp.maximum(slack, 0))
    moved = jax.random.randint(jax.random.fold_in(own, 4), (count // 2,), 0, 1 << 20) % (slack + 1)
    sizes = sizes.at[donor].add(-moved).at[sink].add(moved)
    labels = jnp.searchsorted(jnp.cumsum(sizes), jnp.arange(rows * top), side="right").astype(jnp.int32)
    grid = labels.reshape(top, rows).T
    grid = grid[jax.random.permutation(jax.random.fold_in(own, 1), rows)]
    offset_by = jax.random.randint(jax.random.fold_in(own, 2), (rows, 1), 0, top)
    return jnp.take_along_axis(grid, (jnp.arange(top)[None, :] + offset_by) % top, axis=1)


def load_shares(amount, total, reach, slope, full):
    loads = [(1 << 20) // math.isqrt(standing ** slope) + 1 for standing in range(1, amount + 1)]
    largest = reach if full else min(reach, max(-(-total // amount), total * loads[0] // sum(loads)))
    least = 1 if total - largest >= amount - 1 else 0
    counts, rest = [largest] + [least] * (amount - 1), total - largest - least * (amount - 1)
    while rest > 0:
        free = [i for i in range(1, amount) if counts[i] < largest] or [i for i in range(1, amount) if counts[i] < reach]
        whole, budget = sum([loads[i] for i in free]), rest
        for i in free:
            addition = min(reach - counts[i], max(1, budget * loads[i] // whole), rest)
            counts[i] = counts[i] + addition
            rest = rest - addition
    return np.array(counts)


def normal_values(stream_key, shape, width, reach, split=(), kind=jnp.bfloat16):
    drawn = width * jax.random.normal(stream_key, shape, jnp.float32)
    if split:
        drawn = drawn * block_scale(stream_key, shape, split, -0.22, 0.18)
    return jnp.clip(drawn, -reach, reach).astype(kind)


def setup_inputs(seed: int = 0) -> dict:
    seeds = jax.random.split(jax.random.key(seed), 6)
    obj = normal_values(seeds[0], (2, NR, NC), 1.0, 6.0, ((1, 8), (2, 16)), jnp.float32)
    probe = normal_values(seeds[1], (2, P_SIZE, P_SIZE), 1.0, 6.0, (), jnp.float32)
    intensity = jnp.clip(jnp.exp(math.log(4.0) - 3.6888794 * jax.random.uniform(seeds[2], (FRAMES, P_SIZE, P_SIZE), jnp.float32) ** block_scale(seeds[2], (FRAMES, P_SIZE, P_SIZE), ((0, 128),), -0.2, 0.2)), 0.1, 4.0)
    dest_keys = jax.random.split(jax.random.fold_in(seeds[3], 1), FRAMES // FRAMES_DEV)
    dest_turns = jax.random.permutation(jax.random.fold_in(seeds[3], 3), FRAMES // FRAMES_DEV)
    dest = jax.vmap(lambda own, number: deal_out(jax.random.fold_in(seeds[3], 2), own, number, FRAMES_DEV, N_GX, 1, CAP, 2))(dest_keys, dest_turns).reshape((FRAMES, 1))
    offsets = place_ends(jax.random.randint(seeds[4], (FRAMES, 2), 0, TILE), jax.random.fold_in(seeds[4], 1), 0, TILE - 1).astype(jnp.int32)
    return {"obj": obj, "probe": probe, "intensity": intensity, "dest": dest, "offsets": offsets}


def tables(frame_size):
    index = jnp.arange(frame_size, dtype=jnp.int32)[:, None] * jnp.arange(frame_size, dtype=jnp.int32)[None, :] % frame_size
    angle = index.astype(jnp.float32) * (2.0 * math.pi / frame_size)
    scale = 1.0 / math.sqrt(frame_size)
    return ((jnp.cos(angle) * scale).astype(jnp.bfloat16), (-jnp.sin(angle) * scale).astype(jnp.bfloat16))

def right_mult(matrix, table):
    return jnp.einsum('bmn,nk->bmk', matrix.astype(jnp.float32), table.astype(jnp.float32))

def left_mult(table, matrix):
    return jnp.einsum('km,bmn->bkn', table.astype(jnp.float32), matrix.astype(jnp.float32))

def transform(exit_re, exit_im, amplitude, table_re, table_im):
    half_re = (right_mult(exit_re, table_re) - right_mult(exit_im, table_im)).astype(jnp.bfloat16)
    half_im = (right_mult(exit_re, table_im) + right_mult(exit_im, table_re)).astype(jnp.bfloat16)
    far_re = left_mult(table_re, half_re) - left_mult(table_im, half_im)
    far_im = left_mult(table_re, half_im) + left_mult(table_im, half_re)
    factor = amplitude / jnp.sqrt(far_re * far_re + far_im * far_im + 1.0) - 1.0
    diff_re = (far_re * factor).astype(jnp.bfloat16)
    diff_im = (far_im * factor).astype(jnp.bfloat16)
    mid_re = (right_mult(diff_re, table_re) + right_mult(diff_im, table_im)).astype(jnp.bfloat16)
    mid_im = (right_mult(diff_im, table_re) - right_mult(diff_re, table_im)).astype(jnp.bfloat16)
    back_re = (left_mult(table_re, mid_re) + left_mult(table_im, mid_im)).astype(jnp.bfloat16)
    back_im = (left_mult(table_re, mid_im) - left_mult(table_im, mid_re)).astype(jnp.bfloat16)
    return (back_re, back_im)

def exit_wave(patch, probe):
    exit_re = (probe[0] * patch[:, 0] - probe[1] * patch[:, 1]).astype(jnp.bfloat16)
    exit_im = (probe[0] * patch[:, 1] + probe[1] * patch[:, 0]).astype(jnp.bfloat16)
    return (exit_re, exit_im)

def object_term(back_re, back_im, probe):
    real_part = probe[0] * back_re.astype(jnp.float32) + probe[1] * back_im.astype(jnp.float32)
    imag_part = probe[0] * back_im.astype(jnp.float32) - probe[1] * back_re.astype(jnp.float32)
    return jnp.stack([real_part, imag_part], axis=1)

def reference(obj, probe, intensity, dest, offsets):
    half_width = P_SIZE // 2
    padded = jnp.pad(obj, ((0, 0), (half_width, half_width), (half_width, half_width)))
    table_re, table_im = tables(P_SIZE)
    frame_ids = jnp.arange(FRAMES, dtype=jnp.int32)
    start_rows = (frame_ids // FRAMES_DEV % N_GY * TILE + offsets[:, 0]).astype(jnp.int32)
    start_cols = (dest[:, 0] * TILE + offsets[:, 1]).astype(jnp.int32)
    blocks = FRAMES // FRAMES_DEV
    inten_blocks = intensity.reshape(blocks, FRAMES_DEV, P_SIZE, P_SIZE)
    row_blocks = start_rows.reshape(blocks, FRAMES_DEV)
    col_blocks = start_cols.reshape(blocks, FRAMES_DEV)
    zero_index = jnp.int32(0)

    def cut(start_row, start_col):
        return lax.dynamic_slice(padded, (zero_index, start_row, start_col), (2, P_SIZE, P_SIZE))

    def block_step(total, inputs):
        inten, rows_here, cols_here = inputs
        patch = jax.vmap(cut)(rows_here, cols_here)
        exit_re, exit_im = exit_wave(patch, probe)
        back_re, back_im = transform(exit_re, exit_im, jnp.sqrt(inten), table_re, table_im)
        terms = object_term(back_re, back_im, probe)

        def add_one(index, running):
            where = (zero_index, rows_here[index], cols_here[index])
            region = lax.dynamic_slice(running, where, (2, P_SIZE, P_SIZE))
            return lax.dynamic_update_slice(running, region + terms[index], where)
        total = lax.fori_loop(0, FRAMES_DEV, add_one, total)
        return (total, None)
    total, unused = lax.scan(block_step, jnp.zeros(padded.shape, jnp.float32), (inten_blocks, row_blocks, col_blocks))
    grad = total[:, half_width:half_width + NR, half_width:half_width + NC]
    return obj + 0.5 * grad
```

```python
import math

import jax
import jax.numpy as jnp
import numpy as np
from jax import lax
from jax.experimental import pallas as pl
from jax.experimental.pallas import tpu as pltpu
from jax.sharding import PartitionSpec as P

CAP = 2
FRAME = 256
HALF = 128
TILE = 512
EXTENT = TILE + 2 * HALF
PANELS = EXTENT // 128
BF16 = jnp.bfloat16
F32 = jnp.float32


def table_blocks():
    index = np.arange(FRAME)[:, None] * np.arange(FRAME)[None, :] % FRAME
    angle = index.astype(np.float32) * np.float32(2.0 * math.pi / FRAME)
    scale = np.float32(1.0 / math.sqrt(FRAME))
    re = (np.cos(angle) * scale).astype(BF16)
    im = (-np.sin(angle) * scale).astype(BF16)
    blocks = []
    for parity in (0, 1):
        c = re[:HALF, parity::2]
        s = im[:HALF, parity::2]
        fwd_right = np.block([[c, s], [-s, c]])
        fwd_left = fwd_right.T
        inv_right = np.block([[c.T, -s.T], [s.T, c.T]])
        inv_left = inv_right.T
        blocks.append([fwd_right, fwd_left, inv_right, inv_left])
    return np.stack([blocks[p][i] for i in range(4) for p in (0, 1)]).astype(BF16)


def deinterleave():
    perm = np.zeros((FRAME, FRAME), np.float32)
    for j in range(HALF):
        perm[2 * j, j] = 1.0
        perm[2 * j + 1, HALF + j] = 1.0
    return np.stack([perm, perm.T]).astype(BF16)


def dot(a, b):
    return jnp.dot(a, b, preferred_element_type=F32)


def prep_kernel(dest_ref, inten_ref, perm_ref, first_ref, second_ref, stage, sems):
    f = pl.program_id(0)
    count = pl.num_programs(0)
    slot = f % 2

    def wait_slot(s):
        pltpu.make_async_copy(stage.at[s], first_ref.at[0], sems.at[s]).wait()

    @pl.when(f >= 2)
    def _():
        wait_slot(slot)

    amp = jnp.sqrt(inten_ref[0]).astype(BF16)
    cols = dot(amp, perm_ref[0]).astype(BF16)
    stage[slot] = dot(perm_ref[1], cols).astype(BF16)
    mine = dest_ref[f]

    def count_same(i, total):
        return total + jnp.where(dest_ref[i] == mine, 1, 0)

    rank = lax.fori_loop(0, f, count_same, 0)

    @pl.when(rank == 0)
    def _():
        pltpu.make_async_copy(stage.at[slot], first_ref.at[mine], sems.at[slot]).start()

    @pl.when(rank != 0)
    def _():
        pltpu.make_async_copy(stage.at[slot], second_ref.at[mine], sems.at[slot]).start()

    @pl.when(f == count - 1)
    def _():
        wait_slot(slot)
        wait_slot(1 - slot)


def prep(dest, intensity, groups):
    frames = intensity.shape[0]
    out = jax.ShapeDtypeStruct((groups, FRAME, FRAME), BF16)
    return pl.pallas_call(
        prep_kernel,
        grid_spec=pltpu.PrefetchScalarGridSpec(
            num_scalar_prefetch=1,
            grid=(frames,),
            in_specs=[
                pl.BlockSpec((1, FRAME, FRAME), lambda f, d: (f, 0, 0)),
                pl.BlockSpec((2, FRAME, FRAME), lambda f, d: (0, 0, 0)),
            ],
            out_specs=[pl.BlockSpec(memory_space=pl.ANY)] * 2,
            scratch_shapes=[
                pltpu.VMEM((2, FRAME, FRAME), BF16),
                pltpu.SemaphoreType.DMA((2,)),
            ],
        ),
        out_shape=[out, out],
        compiler_params=pltpu.CompilerParams(vmem_limit_bytes=16 << 20),
        cost_estimate=pl.CostEstimate(
            flops=frames * 4 * FRAME**3, bytes_accessed=frames * FRAME * FRAME * 6, transcendentals=0
        ),
        name="prep",
    )(dest, intensity, jnp.asarray(deinterleave()))


def assemble_kernel(obj_ref, north_ref, south_ref, west_ref, east_ref, ext_ref):
    for part in range(2):
        ext_ref[part, 0] = west_ref[part].astype(F32)
        ext_ref[part, PANELS - 1] = east_ref[part].astype(F32)
        for j in range(TILE // 128):
            lanes = slice(128 * j, 128 * j + 128)
            ext_ref[part, j + 1, 0:HALF, :] = north_ref[part, :, lanes].astype(F32)
            ext_ref[part, j + 1, HALF : HALF + TILE, :] = obj_ref[part, :, lanes]
            ext_ref[part, j + 1, HALF + TILE :, :] = south_ref[part, :, lanes].astype(F32)


def assemble(obj, north, south, west, east):
    return pl.pallas_call(
        assemble_kernel,
        out_shape=jax.ShapeDtypeStruct((2, PANELS, EXTENT, 128), F32),
        compiler_params=pltpu.CompilerParams(vmem_limit_bytes=24 << 20),
        cost_estimate=pl.CostEstimate(flops=0, bytes_accessed=8 << 20, transcendentals=0),
        name="assemble",
    )(obj, north, south, west, east)


def process(row, col, amp, probe_ref, table_ref, ext_ref, acc_ref, xs, gs, ds, ms):
    panel = col // 128
    shift = col % 128
    back_shift = (128 - shift) % 128
    lane = lax.broadcasted_iota(jnp.int32, (FRAME, 128), 1)
    keep = lane < 128 - shift

    def cut(part):
        rolled = [
            pltpu.roll(ext_ref[part, panel + i, pl.ds(row, FRAME), :], back_shift, 1)
            for i in range(3)
        ]
        return [jnp.where(keep, rolled[i], rolled[i + 1]) for i in range(2)]

    patch_re = cut(0)
    patch_im = cut(1)
    ex_re, ex_im = [], []
    for h in range(2):
        lanes = slice(128 * h, 128 * h + 128)
        pr = probe_ref[0, :, lanes]
        pi = probe_ref[1, :, lanes]
        ex_re.append(pr * patch_re[h] - pi * patch_im[h])
        ex_im.append(pr * patch_im[h] + pi * patch_re[h])
    xs[0, :, 0:128] = (ex_re[0] + ex_re[1]).astype(BF16)
    xs[0, :, 128:256] = (ex_im[0] + ex_im[1]).astype(BF16)
    xs[1, :, 0:128] = (ex_re[0] - ex_re[1]).astype(BF16)
    xs[1, :, 128:256] = (ex_im[0] - ex_im[1]).astype(BF16)
    for q in range(2):
        half = dot(xs[q], table_ref[q])
        top, bottom = half[:HALF], half[HALF:]
        lanes = slice(128 * q, 128 * q + 128)
        for p, fold in ((0, top + bottom), (1, top - bottom)):
            folded = fold.astype(BF16)
            gs[p, 0:HALF, lanes] = folded[:, :128]
            gs[p, HALF:, lanes] = folded[:, 128:]
    for p in range(2):
        far = dot(table_ref[2 + p], gs[p])
        far_re, far_im = far[:HALF], far[HALF:]
        rows = slice(HALF * p, HALF * p + HALF)
        a = amp[rows].astype(F32)
        factor = a * lax.rsqrt(far_re * far_re + far_im * far_im + 1.0) - 1.0
        diff_re = (far_re * factor).astype(BF16)
        diff_im = (far_im * factor).astype(BF16)
        for q in range(2):
            lanes = slice(128 * q, 128 * q + 128)
            ds[q, rows, 0:128] = diff_re[:, lanes]
            ds[q, rows, 128:256] = diff_im[:, lanes]
    even = dot(ds[0], table_ref[4])
    odd = dot(ds[1], table_ref[5])
    for h, mid in ((0, (even + odd).astype(BF16)), (1, (even - odd).astype(BF16))):
        lanes = slice(128 * h, 128 * h + 128)
        for p in range(2):
            rows = slice(HALF * p, HALF * p + HALF)
            ms[p, 0:HALF, lanes] = mid[rows, :128]
            ms[p, HALF:, lanes] = mid[rows, 128:]
    even = dot(table_ref[6], ms[0])
    odd = dot(table_ref[7], ms[1])
    keep = lane[:HALF] < shift
    for v in range(2):
        back = even + odd if v == 0 else even - odd
        back_re, back_im = back[:HALF], back[HALF:]
        rows = slice(HALF * v, HALF * v + HALF)
        pr = probe_ref[0, rows]
        pi = probe_ref[1, rows]
        where = pl.ds(row + HALF * v, HALF)
        for part, term in ((0, pr * back_re + pi * back_im), (1, pr * back_im - pi * back_re)):
            left = pltpu.roll(term[:, :128], shift, 1)
            right = pltpu.roll(term[:, 128:], shift, 1)
            acc_ref[part, panel, where, :] += jnp.where(keep, 0.0, left)
            acc_ref[part, panel + 1, where, :] += jnp.where(keep, left, right)
            acc_ref[part, panel + 2, where, :] += jnp.where(keep, right, 0.0)


def first_kernel(meta_ref, amp_ref, probe_ref, table_ref, ext_ref, acc_ref, xs, gs, ds, ms):
    slot = pl.program_id(0)

    @pl.when(slot == 0)
    def _():
        acc_ref[...] = jnp.zeros_like(acc_ref)

    @pl.when(meta_ref[2, slot] > 0)
    def _():
        process(
            meta_ref[0, slot], meta_ref[1, slot], amp_ref.at[0][...], probe_ref, table_ref,
            ext_ref, acc_ref, xs, gs, ds, ms,
        )


def last_kernel(
    meta_ref, amp_ref, probe_ref, table_ref, ext_ref, start_ref,
    west_ref, east_ref, mid_ref, acc_ref, xs, gs, ds, ms,
):
    slot = pl.program_id(0)

    @pl.when(slot == 0)
    def _():
        acc_ref[...] = start_ref[...]

    @pl.when(meta_ref[2, slot] > 0)
    def _():
        process(
            meta_ref[0, slot], meta_ref[1, slot], amp_ref.at[0][...], probe_ref, table_ref,
            ext_ref, acc_ref, xs, gs, ds, ms,
        )

    @pl.when(slot == pl.num_programs(0) - 1)
    def _():
        for part in range(2):
            west_ref[part] = (0.5 * acc_ref[part, 0]).astype(BF16)
            east_ref[part] = (0.5 * acc_ref[part, PANELS - 1]).astype(BF16)
            for j in range(TILE // 128):
                lanes = slice(128 * j, 128 * j + 128)
                inner = slice(HALF, HALF + TILE)
                mid_ref[part, 0:HALF, lanes] = 0.5 * acc_ref[part, j + 1, 0:HALF, :]
                mid_ref[part, inner, lanes] = (
                    ext_ref[part, j + 1, inner, :] + 0.5 * acc_ref[part, j + 1, inner, :]
                )
                mid_ref[part, HALF + TILE :, lanes] = 0.5 * acc_ref[part, j + 1, HALF + TILE :, :]


def whole(shape):
    return pl.BlockSpec(shape, lambda s, m: (0,) * len(shape))


def run_slots(meta, amps, probe, tabs, ext, acc=None):
    slots = amps.shape[0]
    wide = (2, PANELS, EXTENT, 128)
    in_specs = [
        pl.BlockSpec((1, FRAME, FRAME), lambda s, m: (s, 0, 0)),
        whole((2, FRAME, FRAME)),
        whole((8, FRAME, FRAME)),
        whole(wide),
    ]
    operands = [meta, amps, probe, tabs, ext]
    scratch = [pltpu.VMEM((2, FRAME, FRAME), BF16) for _ in range(4)]
    if acc is None:
        kernel = first_kernel
        out_shape = jax.ShapeDtypeStruct(wide, F32)
        out_specs = whole(wide)
    else:
        kernel = last_kernel
        in_specs.append(whole(wide))
        operands.append(acc)
        shapes = [(2, EXTENT, 128), (2, EXTENT, 128), (2, EXTENT, TILE)]
        out_shape = [jax.ShapeDtypeStruct(s, d) for s, d in zip(shapes, (BF16, BF16, F32))]
        out_specs = [whole(s) for s in shapes]
        scratch = [pltpu.VMEM(wide, F32)] + scratch
    return pl.pallas_call(
        kernel,
        grid_spec=pltpu.PrefetchScalarGridSpec(
            num_scalar_prefetch=1,
            grid=(slots,),
            in_specs=in_specs,
            out_specs=out_specs,
            scratch_shapes=scratch,
        ),
        out_shape=out_shape,
        compiler_params=pltpu.CompilerParams(vmem_limit_bytes=56 << 20),
        cost_estimate=pl.CostEstimate(
            flops=slots * 16 * FRAME**3, bytes_accessed=16 << 20, transcendentals=0
        ),
        name="slots",
    )(*operands)


def finish_kernel(base_ref, strip_ref, out_ref):
    out_ref[...] = base_ref[...] + strip_ref[0].astype(F32)


def shifted(value, axis, by):
    size = lax.axis_size(axis)
    pairs = [(i, i + by) for i in range(size) if 0 <= i + by < size]
    return lax.ppermute(value, axis, pairs)


def body(obj, probe, intensity, dest, offsets):
    groups = lax.axis_size("gx")
    frames = intensity.shape[0]
    me = lax.axis_index("gx")
    info = lax.all_gather(jnp.concatenate([dest, offsets], axis=1), "gx", axis=0)
    hit = info[:, :, 0] == me
    order = jnp.cumsum(hit.astype(jnp.int32), axis=1)
    metas = []
    for rank in range(CAP):
        pick = (hit & (order == rank + 1)).astype(jnp.int32)
        metas.append(
            jnp.stack(
                [
                    jnp.sum(pick * info[:, :, 1], axis=1),
                    jnp.sum(pick * info[:, :, 2], axis=1),
                    jnp.sum(pick, axis=1),
                ]
            )
        )
    sends = prep(dest[:, 0], intensity, groups)
    north = shifted(obj[:, TILE - HALF :, :].astype(BF16), "gy", 1)
    south = shifted(obj[:, :HALF, :].astype(BF16), "gy", -1)
    amps = [lax.all_to_all(s, "gx", split_axis=0, concat_axis=0, tiled=True) for s in sends]

    def column(lo, hi):
        own = obj[:, :, lo:hi].astype(BF16)
        return jnp.concatenate([north[:, :, lo:hi], own, south[:, :, lo:hi]], axis=1)

    west = shifted(column(TILE - HALF, TILE), "gx", 1)
    east = shifted(column(0, HALF), "gx", -1)
    ext = assemble(obj, north, south, west, east)
    tabs = jnp.asarray(table_blocks())
    acc = run_slots(metas[0], amps[0], probe, tabs, ext)
    west, east, mid = run_slots(metas[1], amps[1], probe, tabs, ext, acc)
    from_west = shifted(east, "gx", 1).astype(F32)
    from_east = shifted(west, "gx", -1).astype(F32)

    def summed(lo, hi):
        rows = mid[:, lo:hi]
        left = rows[:, :, :HALF] + from_west[:, lo:hi]
        right = rows[:, :, TILE - HALF :] + from_east[:, lo:hi]
        return jnp.concatenate([left, rows[:, :, HALF : TILE - HALF], right], axis=2)

    to_north = summed(0, HALF).astype(BF16)
    to_south = summed(HALF + TILE, EXTENT).astype(BF16)
    from_north = shifted(to_south, "gy", 1)
    from_south = shifted(to_north, "gy", -1)
    inner = summed(HALF, HALF + TILE)
    strips = jnp.stack([from_north, from_south])
    return pl.pallas_call(
        finish_kernel,
        grid=(2,),
        in_specs=[
            pl.BlockSpec((2, HALF, TILE), lambda i: (0, 3 * i, 0)),
            pl.BlockSpec((1, 2, HALF, TILE), lambda i: (i, 0, 0, 0)),
        ],
        out_specs=pl.BlockSpec((2, HALF, TILE), lambda i: (0, 3 * i, 0)),
        out_shape=jax.ShapeDtypeStruct((2, TILE, TILE), F32),
        input_output_aliases={0: 0},
        name="finish",
    )(inner, strips)


def solution(mesh):
    placed = (
        P(None, "gy", "gx"),
        P(),
        P(("gx", "gy"), None, None),
        P(("gx", "gy"), None),
        P(("gx", "gy"), None),
    )
    return jax.shard_map(
        body, mesh=mesh, in_specs=placed, out_specs=P(None, "gy", "gx"), check_vma=False
    )
```

```python
import math

import jax
import jax.numpy as jnp
import numpy as np
from jax import lax
from jax.experimental import pallas as pl
from jax.experimental.pallas import tpu as pltpu
from jax.sharding import PartitionSpec as P

CAP = 2
FRAME = 256
HALF = 128
TILE = 512
EXTENT = TILE + 2 * HALF
PANELS = EXTENT // 128
NOTE_ROWS = 16
GROUP = 4
BF16 = jnp.bfloat16
F32 = jnp.float32


def table_blocks():
    index = np.arange(FRAME)[:, None] * np.arange(FRAME)[None, :] % FRAME
    angle = index.astype(np.float32) * np.float32(2.0 * math.pi / FRAME)
    scale = np.float32(1.0 / math.sqrt(FRAME))
    re = (np.cos(angle) * scale).astype(BF16)
    im = (-np.sin(angle) * scale).astype(BF16)
    blocks = []
    for parity in (0, 1):
        c = re[:HALF, parity::2]
        s = im[:HALF, parity::2]
        fwd_right = np.block([[c, s], [-s, c]])
        fwd_left = fwd_right.T
        inv_right = np.block([[c.T, -s.T], [s.T, c.T]])
        inv_left = inv_right.T
        blocks.append([fwd_right, fwd_left, inv_right, inv_left])
    return np.stack([blocks[p][i] for i in range(4) for p in (0, 1)]).astype(BF16)


def deinterleave():
    perm = np.zeros((FRAME, FRAME), np.float32)
    for j in range(HALF):
        perm[2 * j, j] = 1.0
        perm[2 * j + 1, HALF + j] = 1.0
    return perm.astype(BF16)


def dot(a, b):
    return jnp.dot(a, b, preferred_element_type=F32)


def prep_kernel(dest_ref, offs_ref, left_ref, right_ref, perm_ref, first_ref, second_ref, stage, notes, ranks, sems):
    step = pl.program_id(0)
    count = pl.num_programs(0)
    per = left_ref.shape[0]
    groups = first_ref.shape[0]
    slot = step % 2

    def notes_copy():
        return pltpu.make_async_copy(
            notes, first_ref.at[:, pl.ds(2 * FRAME, NOTE_ROWS), :], sems.at[2 * per]
        )

    @pl.when(step == 0)
    def _():
        lane = lax.broadcasted_iota(jnp.int32, (1, 1, 128), 2)
        owner = lax.broadcasted_iota(jnp.int32, (groups, 1, 128), 0)
        lane = jnp.broadcast_to(lane, (groups, 1, 128))
        note = jnp.zeros((groups, 1, 128), jnp.int32)
        for g in range(groups):
            ranks[per * count + g] = 0
        for f in range(per * count):
            mine = dest_ref[f]
            rank = ranks[per * count + mine]
            ranks[f] = rank
            ranks[per * count + mine] = rank + 1
            row, col = offs_ref[2 * f], offs_ref[2 * f + 1]
            at = lane - 5 * rank
            value = jnp.where(at == 0, row // 16, jnp.where(at == 1, row % 16, 0))
            value += jnp.where(at == 2, col // 16, jnp.where(at == 3, col % 16, 0))
            value += jnp.where(at == 4, 1, 0)
            note = jnp.where(owner == mine, note + value, note)
        notes[...] = jnp.broadcast_to(note.astype(F32), notes.shape).astype(BF16)
        notes_copy().start()

    for i in range(per):

        @pl.when(step >= 2)
        def _():
            pltpu.make_async_copy(
                stage.at[slot, i], second_ref.at[0], sems.at[slot * per + i]
            ).wait()

    for i in range(per):
        rows = [
            jnp.concatenate([ref[i, pl.ds(p, HALF, 2), :] for ref in (left_ref, right_ref)], axis=1)
            for p in range(2)
        ]
        amp = jnp.sqrt(jnp.concatenate(rows, axis=0)).astype(BF16)
        cols = dot(amp, perm_ref[...]).astype(BF16)
        stage[slot, i, 0:FRAME, :] = cols[:, :128]
        stage[slot, i, FRAME : 2 * FRAME, :] = cols[:, 128:]
    for i in range(per):
        f = step * per + i
        mine = dest_ref[f]
        rank = ranks[f]

        @pl.when(rank == 0)
        def _():
            pltpu.make_async_copy(
                stage.at[slot, i],
                first_ref.at[mine, pl.ds(0, 2 * FRAME), :],
                sems.at[slot * per + i],
            ).start()

        @pl.when(rank != 0)
        def _():
            pltpu.make_async_copy(
                stage.at[slot, i], second_ref.at[mine], sems.at[slot * per + i]
            ).start()

    @pl.when(step == count - 1)
    def _():
        notes_copy().wait()
        for s in range(2):
            for i in range(per):
                pltpu.make_async_copy(
                    stage.at[s, i], second_ref.at[0], sems.at[s * per + i]
                ).wait()


def prep(dest, offsets, intensity, groups):
    frames = intensity.shape[0]
    per = 2
    return pl.pallas_call(
        prep_kernel,
        grid_spec=pltpu.PrefetchScalarGridSpec(
            num_scalar_prefetch=2,
            grid=(frames // per,),
            in_specs=[
                pl.BlockSpec((per, FRAME, 128), lambda s, d, o: (s, 0, 0)),
                pl.BlockSpec((per, FRAME, 128), lambda s, d, o: (s, 0, 1)),
                pl.BlockSpec((FRAME, FRAME), lambda s, d, o: (0, 0)),
            ],
            out_specs=[pl.BlockSpec(memory_space=pl.ANY)] * 2,
            scratch_shapes=[
                pltpu.VMEM((2, per, 2 * FRAME, 128), BF16),
                pltpu.VMEM((groups, NOTE_ROWS, 128), BF16),
                pltpu.SMEM((frames + groups,), jnp.int32),
                pltpu.SemaphoreType.DMA((2 * per + 1,)),
            ],
        ),
        out_shape=[
            jax.ShapeDtypeStruct((groups, 2 * FRAME + NOTE_ROWS, 128), BF16),
            jax.ShapeDtypeStruct((groups, 2 * FRAME, 128), BF16),
        ],
        compiler_params=pltpu.CompilerParams(vmem_limit_bytes=56 << 20),
        cost_estimate=pl.CostEstimate(
            flops=frames * 2 * FRAME**3, bytes_accessed=frames * FRAME * FRAME * 6, transcendentals=0
        ),
        name="prep",
    )(dest, offsets, intensity, intensity, jnp.asarray(deinterleave()))


def assemble_kernel(obj_ref, north_ref, south_ref, west_ref, east_ref, ext_ref):
    for part in range(2):
        ext_ref[part, 0] = west_ref[part].astype(F32)
        ext_ref[part, PANELS - 1] = east_ref[part].astype(F32)
        for j in range(TILE // 128):
            lanes = slice(128 * j, 128 * j + 128)
            ext_ref[part, j + 1, 0:HALF, :] = north_ref[part, :, lanes].astype(F32)
            ext_ref[part, j + 1, HALF : HALF + TILE, :] = obj_ref[part, :, lanes]
            ext_ref[part, j + 1, HALF + TILE :, :] = south_ref[part, :, lanes].astype(F32)


def assemble(obj, north, south, west, east):
    return pl.pallas_call(
        assemble_kernel,
        out_shape=jax.ShapeDtypeStruct((2, PANELS, EXTENT, 128), F32),
        compiler_params=pltpu.CompilerParams(vmem_limit_bytes=24 << 20),
        cost_estimate=pl.CostEstimate(flops=0, bytes_accessed=8 << 20, transcendentals=0),
        name="assemble",
    )(obj, north, south, west, east)


def process(places, amp_ref, probe_ref, table_ref, ext_ref, acc_ref, xs, gs, ds, ms):
    members = range(len(places))
    lane = lax.broadcasted_iota(jnp.int32, (FRAME, 128), 1)
    rows_of = [slice(FRAME * m, FRAME * m + FRAME) for m in members]
    for m in members:
        row, col, live = places[m]
        panel = col // 128
        shift = col % 128
        back_shift = (128 - shift) % 128
        keep = lane < 128 - shift

        def cut(part):
            rolled = [
                pltpu.roll(ext_ref[part, panel + i, pl.ds(row, FRAME), :], back_shift, 1)
                for i in range(3)
            ]
            return [jnp.where(keep, rolled[i], rolled[i + 1]) for i in range(2)]

        patch_re = cut(0)
        patch_im = cut(1)
        ex_re, ex_im = [], []
        for h in range(2):
            lanes = slice(128 * h, 128 * h + 128)
            pr = probe_ref[0, :, lanes]
            pi = probe_ref[1, :, lanes]
            ex_re.append(pr * patch_re[h] - pi * patch_im[h])
            ex_im.append(pr * patch_im[h] + pi * patch_re[h])
        xs[0, rows_of[m], 0:128] = (ex_re[0] + ex_re[1]).astype(BF16)
        xs[0, rows_of[m], 128:256] = (ex_im[0] + ex_im[1]).astype(BF16)
        xs[1, rows_of[m], 0:128] = (ex_re[0] - ex_re[1]).astype(BF16)
        xs[1, rows_of[m], 128:256] = (ex_im[0] - ex_im[1]).astype(BF16)
    halves = [dot(xs[q], table_ref[q]) for q in range(2)]
    for m in members:
        for q in range(2):
            half = halves[q][rows_of[m]]
            top, bottom = half[:HALF], half[HALF:]
            lanes = slice(128 * q, 128 * q + 128)
            for p, fold in ((0, top + bottom), (1, top - bottom)):
                folded = fold.astype(BF16)
                gs[m, p, 0:HALF, lanes] = folded[:, :128]
                gs[m, p, HALF:, lanes] = folded[:, 128:]
    for m in members:
        for p in range(2):
            far = dot(table_ref[2 + p], gs[m, p])
            rows = slice(FRAME * m + HALF * p, FRAME * m + HALF * p + HALF)
            for q in range(2):
                lanes = slice(128 * q, 128 * q + 128)
                far_re, far_im = far[:HALF, lanes], far[HALF:, lanes]
                a = amp_ref[m, FRAME * q + HALF * p : FRAME * q + HALF * p + HALF, :].astype(F32)
                factor = a * lax.rsqrt(far_re * far_re + far_im * far_im + 1.0) - 1.0
                ds[q, rows, 0:128] = (far_re * factor).astype(BF16)
                ds[q, rows, 128:256] = (far_im * factor).astype(BF16)
    evens = dot(ds[0], table_ref[4])
    odds = dot(ds[1], table_ref[5])
    for m in members:
        even, odd = evens[rows_of[m]], odds[rows_of[m]]
        for h, mid in ((0, (even + odd).astype(BF16)), (1, (even - odd).astype(BF16))):
            lanes = slice(128 * h, 128 * h + 128)
            for p in range(2):
                rows = slice(HALF * p, HALF * p + HALF)
                ms[m, p, 0:HALF, lanes] = mid[rows, :128]
                ms[m, p, HALF:, lanes] = mid[rows, 128:]
    for m in members:
        row, col, live = places[m]
        shift = col % 128
        panel = jnp.where(live > 0, col // 128, PANELS)
        even = dot(table_ref[6], ms[m, 0])
        odd = dot(table_ref[7], ms[m, 1])
        keep = lane[:HALF] < shift
        for v in range(2):
            back = even + odd if v == 0 else even - odd
            back_re, back_im = back[:HALF], back[HALF:]
            rows = slice(HALF * v, HALF * v + HALF)
            pr = probe_ref[0, rows]
            pi = probe_ref[1, rows]
            where = pl.ds(row + HALF * v, HALF)
            for part, term in ((0, pr * back_re + pi * back_im), (1, pr * back_im - pi * back_re)):
                left = pltpu.roll(term[:, :128], shift, 1)
                right = pltpu.roll(term[:, 128:], shift, 1)
                acc_ref[part, panel, where, :] += jnp.where(keep, 0.0, left)
                acc_ref[part, panel + 1, where, :] += jnp.where(keep, left, right)
                acc_ref[part, panel + 2, where, :] += jnp.where(keep, right, 0.0)


def run_group(rank, meta_ref, amp_ref, probe_ref, table_ref, ext_ref, acc_ref, *scratch):
    step = pl.program_id(0)
    places = [[meta_ref[3 * rank + k, step * GROUP + m] for k in range(3)] for m in range(GROUP)]
    live = places[0][2]
    for place in places[1:]:
        live = live + place[2]

    @pl.when(live > 0)
    def _():
        process(places, amp_ref, probe_ref, table_ref, ext_ref, acc_ref, *scratch)


def first_kernel(meta_ref, amp_ref, probe_ref, table_ref, ext_ref, out_ref, acc_ref, *scratch):
    step = pl.program_id(0)

    @pl.when(step == 0)
    def _():
        acc_ref[:, 0:PANELS] = jnp.zeros_like(out_ref)

    run_group(0, meta_ref, amp_ref, probe_ref, table_ref, ext_ref, acc_ref, *scratch)

    @pl.when(step == pl.num_programs(0) - 1)
    def _():
        out_ref[...] = acc_ref[:, 0:PANELS]


def last_kernel(
    meta_ref, amp_ref, probe_ref, table_ref, ext_ref, start_ref,
    west_ref, east_ref, mid_ref, acc_ref, *scratch,
):
    step = pl.program_id(0)

    @pl.when(step == 0)
    def _():
        acc_ref[:, 0:PANELS] = start_ref[...]

    run_group(1, meta_ref, amp_ref, probe_ref, table_ref, ext_ref, acc_ref, *scratch)

    @pl.when(step == pl.num_programs(0) - 1)
    def _():
        for part in range(2):
            west_ref[part] = (0.5 * acc_ref[part, 0]).astype(BF16)
            east_ref[part] = (0.5 * acc_ref[part, PANELS - 1]).astype(BF16)
            for j in range(TILE // 128):
                lanes = slice(128 * j, 128 * j + 128)
                inner = slice(HALF, HALF + TILE)
                mid_ref[part, 0:HALF, lanes] = 0.5 * acc_ref[part, j + 1, 0:HALF, :]
                mid_ref[part, inner, lanes] = (
                    ext_ref[part, j + 1, inner, :] + 0.5 * acc_ref[part, j + 1, inner, :]
                )
                mid_ref[part, HALF + TILE :, lanes] = 0.5 * acc_ref[part, j + 1, HALF + TILE :, :]


def whole(shape):
    return pl.BlockSpec(shape, lambda s, m: (0,) * len(shape))


def run_slots(meta, amps, probe, tabs, ext, acc=None):
    slots = amps.shape[0]
    wide = (2, PANELS, EXTENT, 128)
    in_specs = [
        pl.BlockSpec((GROUP,) + amps.shape[1:], lambda s, m: (s, 0, 0)),
        whole((2, FRAME, FRAME)),
        whole((8, FRAME, FRAME)),
        whole(wide),
    ]
    operands = [meta, amps, probe, tabs, ext]
    rows, cols = (2, GROUP * FRAME, FRAME), (GROUP, 2, FRAME, FRAME)
    scratch = [pltpu.VMEM((2, PANELS + 3, EXTENT, 128), F32)]
    scratch += [pltpu.VMEM(shape, BF16) for shape in (rows, cols, rows, cols)]
    if acc is None:
        kernel = first_kernel
        out_shape = jax.ShapeDtypeStruct(wide, F32)
        out_specs = whole(wide)
    else:
        kernel = last_kernel
        in_specs.append(whole(wide))
        operands.append(acc)
        shapes = [(2, EXTENT, 128), (2, EXTENT, 128), (2, EXTENT, TILE)]
        out_shape = [jax.ShapeDtypeStruct(s, d) for s, d in zip(shapes, (BF16, BF16, F32))]
        out_specs = [whole(s) for s in shapes]
    return pl.pallas_call(
        kernel,
        grid_spec=pltpu.PrefetchScalarGridSpec(
            num_scalar_prefetch=1,
            grid=(slots // GROUP,),
            in_specs=in_specs,
            out_specs=out_specs,
            scratch_shapes=scratch,
        ),
        out_shape=out_shape,
        compiler_params=pltpu.CompilerParams(vmem_limit_bytes=56 << 20),
        cost_estimate=pl.CostEstimate(
            flops=slots * 16 * FRAME**3, bytes_accessed=16 << 20, transcendentals=0
        ),
        name="slots",
    )(*operands)


def finish_kernel(base_ref, strip_ref, out_ref):
    out_ref[...] = base_ref[...] + strip_ref[0].astype(F32)


def shifted(value, axis, by):
    size = lax.axis_size(axis)
    pairs = [(i, i + by) for i in range(size) if 0 <= i + by < size]
    return lax.ppermute(value, axis, pairs)


def body(obj, probe, intensity, dest, offsets):
    groups = lax.axis_size("gx")
    sends = prep(dest[:, 0], offsets.reshape(-1), intensity, groups)
    north = shifted(obj[:, TILE - HALF :, :].astype(BF16), "gy", 1)
    south = shifted(obj[:, :HALF, :].astype(BF16), "gy", -1)
    amps = [lax.all_to_all(s, "gx", split_axis=0, concat_axis=0, tiled=True) for s in sends]

    def column(lo, hi):
        own = obj[:, :, lo:hi].astype(BF16)
        return jnp.concatenate([north[:, :, lo:hi], own, south[:, :, lo:hi]], axis=1)

    west = shifted(column(TILE - HALF, TILE), "gx", 1)
    east = shifted(column(0, HALF), "gx", -1)
    ext = assemble(obj, north, south, west, east)
    tabs = jnp.asarray(table_blocks())
    notes = amps[0][:, 2 * FRAME, :10].astype(jnp.int32).T
    meta = jnp.stack(
        [
            notes[5 * r] * 16 + notes[5 * r + 1] if k == 0 else
            notes[5 * r + 2] * 16 + notes[5 * r + 3] if k == 1 else notes[5 * r + 4]
            for r in range(CAP) for k in range(3)
        ]
    )
    acc = run_slots(meta, amps[0], probe, tabs, ext)
    west, east, mid = run_slots(meta, amps[1], probe, tabs, ext, acc)
    from_west = shifted(east, "gx", 1).astype(F32)
    from_east = shifted(west, "gx", -1).astype(F32)

    def summed(lo, hi):
        rows = mid[:, lo:hi]
        left = rows[:, :, :HALF] + from_west[:, lo:hi]
        right = rows[:, :, TILE - HALF :] + from_east[:, lo:hi]
        return jnp.concatenate([left, rows[:, :, HALF : TILE - HALF], right], axis=2)

    to_north = summed(0, HALF).astype(BF16)
    to_south = summed(HALF + TILE, EXTENT).astype(BF16)
    from_north = shifted(to_south, "gy", 1)
    from_south = shifted(to_north, "gy", -1)
    inner = summed(HALF, HALF + TILE)
    strips = jnp.stack([from_north, from_south])
    return pl.pallas_call(
        finish_kernel,
        grid=(2,),
        in_specs=[
            pl.BlockSpec((2, HALF, TILE), lambda i: (0, 3 * i, 0)),
            pl.BlockSpec((1, 2, HALF, TILE), lambda i: (i, 0, 0, 0)),
        ],
        out_specs=pl.BlockSpec((2, HALF, TILE), lambda i: (0, 3 * i, 0)),
        out_shape=jax.ShapeDtypeStruct((2, TILE, TILE), F32),
        input_output_aliases={0: 0},
        name="finish",
    )(inner, strips)


def solution(mesh):
    placed = (
        P(None, "gy", "gx"),
        P(),
        P(("gx", "gy"), None, None),
        P(("gx", "gy"), None),
        P(("gx", "gy"), None),
    )
    return jax.shard_map(
        body, mesh=mesh, in_specs=placed, out_specs=P(None, "gy", "gx"), check_vma=False
    )
```

```python
import functools
import math

import jax
import jax.numpy as jnp
import numpy as np
from jax import lax
from jax.experimental import pallas as pl
from jax.experimental.pallas import tpu as pltpu
from jax.sharding import PartitionSpec as P

CAP = 2
FRAME = 256
HALF = 128
TILE = 512
EXTENT = TILE + 2 * HALF
PANELS = EXTENT // 128
NOTE_ROWS = 16
GROUP = 4
BF16 = jnp.bfloat16
F32 = jnp.float32


def table_blocks():
    index = np.arange(FRAME)[:, None] * np.arange(FRAME)[None, :] % FRAME
    angle = index.astype(np.float32) * np.float32(2.0 * math.pi / FRAME)
    scale = np.float32(1.0 / math.sqrt(FRAME))
    re = (np.cos(angle) * scale).astype(BF16)
    im = (-np.sin(angle) * scale).astype(BF16)
    blocks = []
    for parity in (0, 1):
        c = re[:HALF, parity::2]
        s = im[:HALF, parity::2]
        fwd_right = np.block([[c, s], [-s, c]])
        fwd_left = fwd_right.T
        inv_right = np.block([[c.T, -s.T], [s.T, c.T]])
        inv_left = inv_right.T
        blocks.append([fwd_right, fwd_left, inv_right, inv_left])
    return np.stack([blocks[p][i] for i in range(4) for p in (0, 1)]).astype(BF16)


def deinterleave():
    perm = np.zeros((FRAME, FRAME), np.float32)
    for j in range(HALF):
        perm[2 * j, j] = 1.0
        perm[2 * j + 1, HALF + j] = 1.0
    return perm.astype(BF16)


def dot(a, b):
    return jnp.dot(a, b, preferred_element_type=F32)


def prep_kernel(
    where_ref, inten_ref, perm_ref, first_ref, second_ref, stage, split, notes, ranks, sems
):
    step = pl.program_id(0)
    count = pl.num_programs(0)
    per = inten_ref.shape[0]
    groups = first_ref.shape[0]
    slot = step % 2

    def notes_copy():
        return pltpu.make_async_copy(
            notes, first_ref.at[:, pl.ds(2 * FRAME, NOTE_ROWS), :], sems.at[2 * per]
        )

    @pl.when(step == 0)
    def _():
        lane = lax.broadcasted_iota(jnp.int32, (groups, 128), 1)
        owner = lax.broadcasted_iota(jnp.int32, (groups, 128), 0)
        note = jnp.zeros((groups, 128), jnp.int32)
        for g in range(groups):
            ranks[per * count + g] = 0
        for f in range(per * count):
            mine = where_ref[f]
            rank = ranks[per * count + mine]
            ranks[f] = rank
            ranks[per * count + mine] = rank + 1
            row, col = where_ref[per * count + f], where_ref[2 * per * count + f]
            at = lane - 5 * rank
            value = jnp.where(at == 0, row // 16, jnp.where(at == 1, row % 16, 0))
            value += jnp.where(at == 2, col // 16, jnp.where(at == 3, col % 16, 0))
            value += jnp.where(at == 4, 1, 0)
            note = jnp.where(owner == mine, note + value, note)
        notes[...] = jnp.broadcast_to(note.astype(F32)[:, None, :], notes.shape).astype(BF16)
        notes_copy().start()

    for i in range(per):

        @pl.when(step >= 2)
        def _():
            pltpu.make_async_copy(
                stage.at[slot, i], second_ref.at[0], sems.at[slot * per + i]
            ).wait()

    for i in range(per):
        for h in range(2):
            split[i, h] = jnp.sqrt(inten_ref[i, :, 128 * h : 128 * h + 128])
        rows = [
            jnp.concatenate([split[i, h, pl.ds(p, HALF, 2), :] for h in range(2)], axis=1)
            for p in range(2)
        ]
        amp = jnp.concatenate(rows, axis=0).astype(BF16)
        cols = dot(amp, perm_ref[...]).astype(BF16)
        stage[slot, i, 0:FRAME, :] = cols[:, :128]
        stage[slot, i, FRAME : 2 * FRAME, :] = cols[:, 128:]
    for i in range(per):
        f = step * per + i
        mine = where_ref[f]
        rank = ranks[f]

        @pl.when(rank == 0)
        def _():
            pltpu.make_async_copy(
                stage.at[slot, i],
                first_ref.at[mine, pl.ds(0, 2 * FRAME), :],
                sems.at[slot * per + i],
            ).start()

        @pl.when(rank != 0)
        def _():
            pltpu.make_async_copy(
                stage.at[slot, i], second_ref.at[mine], sems.at[slot * per + i]
            ).start()

    @pl.when(step == count - 1)
    def _():
        notes_copy().wait()
        for s in range(2):
            for i in range(per):
                pltpu.make_async_copy(
                    stage.at[s, i], second_ref.at[0], sems.at[s * per + i]
                ).wait()


def prep(where, intensity, groups):
    frames = intensity.shape[0]
    per = 4
    return pl.pallas_call(
        prep_kernel,
        grid_spec=pltpu.PrefetchScalarGridSpec(
            num_scalar_prefetch=1,
            grid=(frames // per,),
            in_specs=[
                pl.BlockSpec((per, FRAME, FRAME), lambda s, w: (s, 0, 0)),
                pl.BlockSpec((FRAME, FRAME), lambda s, w: (0, 0)),
            ],
            out_specs=[pl.BlockSpec(memory_space=pl.ANY)] * 2,
            scratch_shapes=[
                pltpu.VMEM((2, per, 2 * FRAME, 128), BF16),
                pltpu.VMEM((per, 2, FRAME, 128), F32),
                pltpu.VMEM((groups, NOTE_ROWS, 128), BF16),
                pltpu.SMEM((frames + groups,), jnp.int32),
                pltpu.SemaphoreType.DMA((2 * per + 1,)),
            ],
        ),
        out_shape=[
            jax.ShapeDtypeStruct((groups, 2 * FRAME + NOTE_ROWS, 128), BF16),
            jax.ShapeDtypeStruct((groups, 2 * FRAME, 128), BF16),
        ],
        compiler_params=pltpu.CompilerParams(vmem_limit_bytes=56 << 20),
        cost_estimate=pl.CostEstimate(
            flops=frames * 2 * FRAME**3, bytes_accessed=frames * FRAME * FRAME * 6, transcendentals=0
        ),
        name="prep",
    )(where, intensity, jnp.asarray(deinterleave()))


def assemble_kernel(obj_ref, north_ref, south_ref, west_ref, east_ref, ext_ref):
    for part in range(2):
        ext_ref[part, 0] = west_ref[part].astype(F32)
        ext_ref[part, PANELS - 1] = east_ref[part].astype(F32)
        for j in range(TILE // 128):
            lanes = slice(128 * j, 128 * j + 128)
            ext_ref[part, j + 1, 0:HALF, :] = north_ref[part, :, lanes].astype(F32)
            ext_ref[part, j + 1, HALF : HALF + TILE, :] = obj_ref[part, :, lanes]
            ext_ref[part, j + 1, HALF + TILE :, :] = south_ref[part, :, lanes].astype(F32)


def assemble(obj, north, south, west, east):
    return pl.pallas_call(
        assemble_kernel,
        out_shape=jax.ShapeDtypeStruct((2, PANELS, EXTENT, 128), F32),
        compiler_params=pltpu.CompilerParams(vmem_limit_bytes=24 << 20),
        cost_estimate=pl.CostEstimate(flops=0, bytes_accessed=8 << 20, transcendentals=0),
        name="assemble",
    )(obj, north, south, west, east)


def rows_of(m, p=0, height=FRAME):
    return slice(FRAME * m + HALF * p, FRAME * m + HALF * p + height)


def forward(places, probe_ref, table_ref, ext_ref, xs, gs, take):
    members = range(len(places))
    lane = lax.broadcasted_iota(jnp.int32, (FRAME, 128), 1)
    for m in members:
        row, col, live = places[m]
        panel = col // 128
        shift = col % 128
        back_shift = (128 - shift) % 128
        keep = lane < 128 - shift

        def cut(part):
            rolled = [
                pltpu.roll(ext_ref[part, panel + i, pl.ds(row, FRAME), :], back_shift, 1)
                for i in range(3)
            ]
            return [jnp.where(keep, rolled[i], rolled[i + 1]) for i in range(2)]

        patch_re = cut(0)
        patch_im = cut(1)
        ex_re, ex_im = [], []
        for h in range(2):
            lanes = slice(128 * h, 128 * h + 128)
            pr = probe_ref[0, :, lanes]
            pi = probe_ref[1, :, lanes]
            ex_re.append(pr * patch_re[h] - pi * patch_im[h])
            ex_im.append(pr * patch_im[h] + pi * patch_re[h])
        xs[0, rows_of(m), 0:128] = (ex_re[0] + ex_re[1]).astype(BF16)
        xs[0, rows_of(m), 128:256] = (ex_im[0] + ex_im[1]).astype(BF16)
        xs[1, rows_of(m), 0:128] = (ex_re[0] - ex_re[1]).astype(BF16)
        xs[1, rows_of(m), 128:256] = (ex_im[0] - ex_im[1]).astype(BF16)
    halves = [dot(xs[q], table_ref[q]) for q in range(2)]
    for m in members:
        for q in range(2):
            half = halves[q][rows_of(m)]
            top, bottom = half[:HALF], half[HALF:]
            lanes = slice(128 * q, 128 * q + 128)
            for p, fold in ((0, top + bottom), (1, top - bottom)):
                folded = fold.astype(BF16)
                gs[m, p, 0:HALF, lanes] = folded[:, :128]
                gs[m, p, HALF:, lanes] = folded[:, 128:]
    for m in members:
        for p in range(2):
            take(m, p, dot(table_ref[2 + p], gs[m, p]))


def update(m, p, far, amp_ref, ds):
    for q in range(2):
        lanes = slice(128 * q, 128 * q + 128)
        far_re, far_im = far[:HALF, lanes], far[HALF:, lanes]
        a = amp_ref[m, FRAME * q + HALF * p : FRAME * q + HALF * p + HALF, :].astype(F32)
        factor = a * lax.rsqrt(far_re * far_re + far_im * far_im + 1.0) - 1.0
        ds[q, rows_of(m, p, HALF), 0:128] = (far_re * factor).astype(BF16)
        ds[q, rows_of(m, p, HALF), 128:256] = (far_im * factor).astype(BF16)


def backward(places, probe_ref, table_ref, acc_ref, ds, ms):
    members = range(len(places))
    lane = lax.broadcasted_iota(jnp.int32, (HALF, 128), 1)
    evens = dot(ds[0], table_ref[4])
    odds = dot(ds[1], table_ref[5])
    for m in members:
        even, odd = evens[rows_of(m)], odds[rows_of(m)]
        for h, mid in ((0, (even + odd).astype(BF16)), (1, (even - odd).astype(BF16))):
            lanes = slice(128 * h, 128 * h + 128)
            for p in range(2):
                rows = slice(HALF * p, HALF * p + HALF)
                ms[m, p, 0:HALF, lanes] = mid[rows, :128]
                ms[m, p, HALF:, lanes] = mid[rows, 128:]
    for m in members:
        row, col, live = places[m]
        shift = col % 128
        panel = jnp.where(live > 0, col // 128, PANELS)
        even = dot(table_ref[6], ms[m, 0])
        odd = dot(table_ref[7], ms[m, 1])
        keep = lane < shift
        for v in range(2):
            back = even + odd if v == 0 else even - odd
            back_re, back_im = back[:HALF], back[HALF:]
            rows = slice(HALF * v, HALF * v + HALF)
            pr = probe_ref[0, rows]
            pi = probe_ref[1, rows]
            where = pl.ds(row + HALF * v, HALF)
            for part, term in ((0, pr * back_re + pi * back_im), (1, pr * back_im - pi * back_re)):
                left = pltpu.roll(term[:, :128], shift, 1)
                right = pltpu.roll(term[:, 128:], shift, 1)
                acc_ref[part, panel, where, :] += jnp.where(keep, 0.0, left)
                acc_ref[part, panel + 1, where, :] += jnp.where(keep, left, right)
                acc_ref[part, panel + 2, where, :] += jnp.where(keep, right, 0.0)


def places_of(meta_ref, rank, group):
    places = [[meta_ref[3 * rank + k, group * GROUP + m] for k in range(3)] for m in range(GROUP)]
    live = places[0][2]
    for place in places[1:]:
        live = live + place[2]
    return places, live > 0


def first_kernel(
    meta_ref, amp_ref, probe_ref, table_ref, ext_ref, out_ref, far_ref, acc_ref, xs, gs, ds, ms
):
    step = pl.program_id(0)
    groups = pl.num_programs(0) // 2

    @pl.when(step == 0)
    def _():
        acc_ref[:, 0:PANELS] = jnp.zeros_like(out_ref)

    places, live = places_of(meta_ref, 0, jnp.minimum(step, groups - 1))

    @pl.when(live & (step < groups))
    def _():
        def take(m, p, far):
            update(m, p, far, amp_ref, ds)

        forward(places, probe_ref, table_ref, ext_ref, xs, gs, take)
        backward(places, probe_ref, table_ref, acc_ref, ds, ms)

    @pl.when(step == groups - 1)
    def _():
        out_ref[...] = acc_ref[:, 0:PANELS]

    later, live = places_of(meta_ref, 1, jnp.maximum(step - groups, 0))

    @pl.when(live & (step >= groups))
    def _():
        def take(m, p, far):
            far_ref[m, p] = far

        forward(later, probe_ref, table_ref, ext_ref, xs, gs, take)


def last_kernel(
    meta_ref, amp_ref, far_ref, probe_ref, table_ref, start_hbm, obj_hbm,
    west_ref, east_ref, mid_ref, acc_ref, start_ref, obj_ref, sems, ds, ms,
):
    step = pl.program_id(0)

    def loads():
        return [
            pltpu.make_async_copy(start_hbm, start_ref, sems.at[0]),
            pltpu.make_async_copy(obj_hbm, obj_ref, sems.at[1]),
        ]

    @pl.when(step == 0)
    def _():
        for copy in loads():
            copy.start()
        acc_ref[:, 0:PANELS] = jnp.zeros_like(start_ref)

    places, live = places_of(meta_ref, 1, step)

    @pl.when(live)
    def _():
        for m in range(GROUP):
            for p in range(2):
                update(m, p, far_ref[m, p], amp_ref, ds)
        backward(places, probe_ref, table_ref, acc_ref, ds, ms)

    @pl.when(step == pl.num_programs(0) - 1)
    def _():
        for copy in loads():
            copy.wait()

        def half_sum(part, panel, rows):
            return 0.5 * (acc_ref[part, panel, rows, :] + start_ref[part, panel, rows, :])

        for part in range(2):
            west_ref[part] = half_sum(part, 0, slice(0, EXTENT)).astype(BF16)
            east_ref[part] = half_sum(part, PANELS - 1, slice(0, EXTENT)).astype(BF16)
            for j in range(TILE // 128):
                lanes = slice(128 * j, 128 * j + 128)
                inner = slice(HALF, HALF + TILE)
                for rows in (slice(0, HALF), slice(HALF + TILE, EXTENT)):
                    mid_ref[part, rows, lanes] = half_sum(part, j + 1, rows)
                mid_ref[part, inner, lanes] = obj_ref[part, :, lanes] + half_sum(part, j + 1, inner)


def whole(shape):
    return pl.BlockSpec(shape, lambda s, m: (0,) * len(shape))


WIDE = (2, PANELS, EXTENT, 128)
SUMS = (2, PANELS + 3, EXTENT, 128)
FLAT = (2, GROUP * FRAME, FRAME)
DEEP = (GROUP, 2, FRAME, FRAME)


def run_first(meta, amps, probe, tabs, ext):
    groups = amps.shape[0] // GROUP
    return pl.pallas_call(
        first_kernel,
        grid_spec=pltpu.PrefetchScalarGridSpec(
            num_scalar_prefetch=1,
            grid=(2 * groups,),
            in_specs=[
                pl.BlockSpec(
                    (GROUP,) + amps.shape[1:], lambda s, m: (jnp.minimum(s, groups - 1), 0, 0)
                ),
                whole((2, FRAME, FRAME)),
                whole((8, FRAME, FRAME)),
                whole(WIDE),
            ],
            out_specs=[
                whole(WIDE),
                pl.BlockSpec(DEEP, lambda s, m: (jnp.maximum(s - groups, 0), 0, 0, 0)),
            ],
            scratch_shapes=[pltpu.VMEM(SUMS, F32)]
            + [pltpu.VMEM(shape, BF16) for shape in (FLAT, DEEP, FLAT, DEEP)],
        ),
        out_shape=[
            jax.ShapeDtypeStruct(WIDE, F32),
            jax.ShapeDtypeStruct((amps.shape[0], 2, FRAME, FRAME), F32),
        ],
        compiler_params=pltpu.CompilerParams(vmem_limit_bytes=56 << 20),
        cost_estimate=pl.CostEstimate(
            flops=2 * amps.shape[0] * 16 * FRAME**3, bytes_accessed=24 << 20, transcendentals=0
        ),
        name="first",
    )(meta, amps, probe, tabs, ext)


def run_last(meta, amps, far, probe, tabs, start, obj):
    groups = amps.shape[0] // GROUP
    shapes = [(2, EXTENT, 128), (2, EXTENT, 128), (2, EXTENT, TILE)]
    return pl.pallas_call(
        last_kernel,
        grid_spec=pltpu.PrefetchScalarGridSpec(
            num_scalar_prefetch=1,
            grid=(groups,),
            in_specs=[
                pl.BlockSpec((GROUP,) + amps.shape[1:], lambda s, m: (s, 0, 0)),
                pl.BlockSpec(DEEP, lambda s, m: (s, 0, 0, 0)),
                whole((2, FRAME, FRAME)),
                whole((8, FRAME, FRAME)),
                pl.BlockSpec(memory_space=pl.ANY),
                pl.BlockSpec(memory_space=pl.ANY),
            ],
            out_specs=[whole(shape) for shape in shapes],
            scratch_shapes=[
                pltpu.VMEM(SUMS, F32),
                pltpu.VMEM(WIDE, F32),
                pltpu.VMEM((2, TILE, TILE), F32),
                pltpu.SemaphoreType.DMA((2,)),
                pltpu.VMEM(FLAT, BF16),
                pltpu.VMEM(DEEP, BF16),
            ],
        ),
        out_shape=[jax.ShapeDtypeStruct(s, d) for s, d in zip(shapes, (BF16, BF16, F32))],
        compiler_params=pltpu.CompilerParams(vmem_limit_bytes=56 << 20),
        cost_estimate=pl.CostEstimate(
            flops=amps.shape[0] * 8 * FRAME**3, bytes_accessed=20 << 20, transcendentals=0
        ),
        name="last",
    )(meta, amps, far, probe, tabs, start, obj)


def finish_kernel(base_ref, north_ref, south_ref, out_ref):
    @pl.when(pl.program_id(0) == 0)
    def _():
        out_ref[...] = base_ref[...] + north_ref[...].astype(F32)

    @pl.when(pl.program_id(0) == 1)
    def _():
        out_ref[...] = base_ref[...] + south_ref[...].astype(F32)


def shifted(value, axis, by):
    size = lax.axis_size(axis)
    pairs = [(i, i + by) for i in range(size) if 0 <= i + by < size]
    return lax.ppermute(value, axis, pairs)


def body(obj, probe, intensity, dest, offsets):
    groups = lax.axis_size("gx")
    sends = prep(jnp.concatenate([dest.T, offsets.T]).reshape(-1), intensity, groups)
    north = shifted(obj[:, TILE - HALF :, :].astype(BF16), "gy", 1)
    south = shifted(obj[:, :HALF, :].astype(BF16), "gy", -1)
    routed = functools.partial(
        lax.all_to_all, axis_name="gx", split_axis=0, concat_axis=0, tiled=True
    )
    amps = routed(sends[0])

    def column(lo, hi):
        own = obj[:, :, lo:hi].astype(BF16)
        return jnp.concatenate([north[:, :, lo:hi], own, south[:, :, lo:hi]], axis=1)

    west = shifted(column(TILE - HALF, TILE), "gx", 1)
    east = shifted(column(0, HALF), "gx", -1)
    west, east, rest = lax.optimization_barrier((west, east, sends[1]))
    more = routed(rest)
    ext = assemble(obj, north, south, west, east)
    tabs = jnp.asarray(table_blocks())
    notes = amps[:, 2 * FRAME, :10].astype(jnp.int32).T
    meta = jnp.stack(
        [
            notes[5 * r] * 16 + notes[5 * r + 1] if k == 0 else
            notes[5 * r + 2] * 16 + notes[5 * r + 3] if k == 1 else notes[5 * r + 4]
            for r in range(CAP) for k in range(3)
        ]
    )
    acc, far = run_first(meta, amps, probe, tabs, ext)
    west, east, mid = run_last(meta, more, far, probe, tabs, acc, obj)
    from_west = shifted(east, "gx", 1).astype(F32)
    from_east = shifted(west, "gx", -1).astype(F32)

    def summed(lo, hi):
        rows = mid[:, lo:hi]
        left = rows[:, :, :HALF] + from_west[:, lo:hi]
        right = rows[:, :, TILE - HALF :] + from_east[:, lo:hi]
        return jnp.concatenate([left, rows[:, :, HALF : TILE - HALF], right], axis=2)

    to_north = summed(0, HALF).astype(BF16)
    to_south = summed(HALF + TILE, EXTENT).astype(BF16)
    from_north = shifted(to_south, "gy", 1)
    from_south = shifted(to_north, "gy", -1)
    inner = summed(HALF, HALF + TILE)
    return pl.pallas_call(
        finish_kernel,
        grid=(2,),
        in_specs=[
            pl.BlockSpec((2, HALF, TILE), lambda i: (0, 3 * i, 0)),
            pl.BlockSpec((2, HALF, TILE), lambda i: (0, 0, 0)),
            pl.BlockSpec((2, HALF, TILE), lambda i: (0, 0, 0)),
        ],
        out_specs=pl.BlockSpec((2, HALF, TILE), lambda i: (0, 3 * i, 0)),
        out_shape=jax.ShapeDtypeStruct((2, TILE, TILE), F32),
        input_output_aliases={0: 0},
        name="finish",
    )(inner, from_north, from_south)


def solution(mesh):
    placed = (
        P(None, "gy", "gx"),
        P(),
        P(("gx", "gy"), None, None),
        P(("gx", "gy"), None),
        P(("gx", "gy"), None),
    )
    return jax.shard_map(
        body, mesh=mesh, in_specs=placed, out_specs=P(None, "gy", "gx"), check_vma=False
    )
```

```python
import functools
import math

import jax
import jax.numpy as jnp
import numpy as np
from jax import lax
from jax.experimental import pallas as pl
from jax.experimental.pallas import tpu as pltpu
from jax.sharding import PartitionSpec as P

CAP = 2
FRAME = 256
HALF = 128
TILE = 512
EXTENT = TILE + 2 * HALF
PANELS = EXTENT // 128
NOTE_ROWS = 16
GROUP = 4
BF16 = jnp.bfloat16
F32 = jnp.float32


def table_blocks():
    index = np.arange(FRAME)[:, None] * np.arange(FRAME)[None, :] % FRAME
    angle = index.astype(np.float32) * np.float32(2.0 * math.pi / FRAME)
    scale = np.float32(1.0 / math.sqrt(FRAME))
    re = (np.cos(angle) * scale).astype(BF16)
    im = (-np.sin(angle) * scale).astype(BF16)
    blocks = []
    for parity in (0, 1):
        c = re[:HALF, parity::2]
        s = im[:HALF, parity::2]
        fwd_right = np.block([[c, s], [-s, c]])
        fwd_left = fwd_right.T
        inv_right = np.block([[c.T, -s.T], [s.T, c.T]])
        inv_left = inv_right.T
        blocks.append([fwd_right, fwd_left, inv_right, inv_left])
    return np.stack([blocks[p][i] for i in range(4) for p in (0, 1)]).astype(BF16)


def deinterleave():
    perm = np.zeros((FRAME, FRAME), np.float32)
    for j in range(HALF):
        perm[2 * j, j] = 1.0
        perm[2 * j + 1, HALF + j] = 1.0
    return perm.astype(BF16)


def dot(a, b):
    return jnp.dot(a, b, preferred_element_type=F32)


def prep_kernel(
    where_ref, inten_ref, perm_ref, first_ref, second_ref, stage, split, notes, ranks, sems
):
    step = pl.program_id(0)
    count = pl.num_programs(0)
    per = inten_ref.shape[0]
    groups = first_ref.shape[0]
    slot = step % 2

    def notes_copy():
        return pltpu.make_async_copy(
            notes, first_ref.at[:, pl.ds(2 * FRAME, NOTE_ROWS), :], sems.at[2 * per]
        )

    @pl.when(step == 0)
    def _():
        lane = lax.broadcasted_iota(jnp.int32, (groups, 128), 1)
        owner = lax.broadcasted_iota(jnp.int32, (groups, 128), 0)
        note = jnp.zeros((groups, 128), jnp.int32)
        for g in range(groups):
            ranks[per * count + g] = 0
        for f in range(per * count):
            mine = where_ref[f]
            rank = ranks[per * count + mine]
            ranks[f] = rank
            ranks[per * count + mine] = rank + 1
            row, col = where_ref[per * count + f], where_ref[2 * per * count + f]
            at = lane - 5 * rank
            value = jnp.where(at == 0, row // 16, jnp.where(at == 1, row % 16, 0))
            value += jnp.where(at == 2, col // 16, jnp.where(at == 3, col % 16, 0))
            value += jnp.where(at == 4, 1, 0)
            note = jnp.where(owner == mine, note + value, note)
        notes[...] = jnp.broadcast_to(note.astype(F32)[:, None, :], notes.shape).astype(BF16)
        notes_copy().start()

    for i in range(per):

        @pl.when(step >= 2)
        def _():
            pltpu.make_async_copy(
                stage.at[slot, i], second_ref.at[0], sems.at[slot * per + i]
            ).wait()

    for i in range(per):
        for h in range(2):
            split[i, h] = jnp.sqrt(inten_ref[i, :, 128 * h : 128 * h + 128])
        rows = [
            jnp.concatenate([split[i, h, pl.ds(p, HALF, 2), :] for h in range(2)], axis=1)
            for p in range(2)
        ]
        amp = jnp.concatenate(rows, axis=0).astype(BF16)
        cols = dot(amp, perm_ref[...]).astype(BF16)
        stage[slot, i, 0:FRAME, :] = cols[:, :128]
        stage[slot, i, FRAME : 2 * FRAME, :] = cols[:, 128:]
    for i in range(per):
        f = step * per + i
        mine = where_ref[f]
        rank = ranks[f]

        @pl.when(rank == 0)
        def _():
            pltpu.make_async_copy(
                stage.at[slot, i],
                first_ref.at[mine, pl.ds(0, 2 * FRAME), :],
                sems.at[slot * per + i],
            ).start()

        @pl.when(rank != 0)
        def _():
            pltpu.make_async_copy(
                stage.at[slot, i], second_ref.at[mine], sems.at[slot * per + i]
            ).start()

    @pl.when(step == count - 1)
    def _():
        notes_copy().wait()
        for s in range(2):
            for i in range(per):
                pltpu.make_async_copy(
                    stage.at[s, i], second_ref.at[0], sems.at[s * per + i]
                ).wait()


def prep(where, intensity, groups):
    frames = intensity.shape[0]
    per = 4
    return pl.pallas_call(
        prep_kernel,
        grid_spec=pltpu.PrefetchScalarGridSpec(
            num_scalar_prefetch=1,
            grid=(frames // per,),
            in_specs=[
                pl.BlockSpec((per, FRAME, FRAME), lambda s, w: (s, 0, 0)),
                pl.BlockSpec((FRAME, FRAME), lambda s, w: (0, 0)),
            ],
            out_specs=[pl.BlockSpec(memory_space=pl.ANY)] * 2,
            scratch_shapes=[
                pltpu.VMEM((2, per, 2 * FRAME, 128), BF16),
                pltpu.VMEM((per, 2, FRAME, 128), F32),
                pltpu.VMEM((groups, NOTE_ROWS, 128), BF16),
                pltpu.SMEM((frames + groups,), jnp.int32),
                pltpu.SemaphoreType.DMA((2 * per + 1,)),
            ],
        ),
        out_shape=[
            jax.ShapeDtypeStruct((groups, 2 * FRAME + NOTE_ROWS, 128), BF16),
            jax.ShapeDtypeStruct((groups, 2 * FRAME, 128), BF16),
        ],
        compiler_params=pltpu.CompilerParams(vmem_limit_bytes=16 << 20),
        cost_estimate=pl.CostEstimate(
            flops=frames * 2 * FRAME**3, bytes_accessed=frames * FRAME * FRAME * 6, transcendentals=0
        ),
        name="prep",
    )(where, intensity, jnp.asarray(deinterleave()))


def assemble_kernel(obj_ref, north_ref, south_ref, west_ref, east_ref, ext_ref):
    for part in range(2):
        ext_ref[part, 0] = west_ref[part].astype(F32)
        ext_ref[part, PANELS - 1] = east_ref[part].astype(F32)
        for j in range(TILE // 128):
            lanes = slice(128 * j, 128 * j + 128)
            ext_ref[part, j + 1, 0:HALF, :] = north_ref[part, :, lanes].astype(F32)
            ext_ref[part, j + 1, HALF : HALF + TILE, :] = obj_ref[part, :, lanes]
            ext_ref[part, j + 1, HALF + TILE :, :] = south_ref[part, :, lanes].astype(F32)


def assemble(obj, north, south, west, east):
    return pl.pallas_call(
        assemble_kernel,
        out_shape=jax.ShapeDtypeStruct((2, PANELS, EXTENT, 128), F32),
        compiler_params=pltpu.CompilerParams(vmem_limit_bytes=24 << 20),
        cost_estimate=pl.CostEstimate(flops=0, bytes_accessed=8 << 20, transcendentals=0),
        name="assemble",
    )(obj, north, south, west, east)


def rows_of(m, p=0, height=FRAME):
    return slice(FRAME * m + HALF * p, FRAME * m + HALF * p + height)


def forward(places, probe_ref, table_ref, ext_ref, xs, gs, take):
    members = range(len(places))
    lane = lax.broadcasted_iota(jnp.int32, (FRAME, 128), 1)
    for m in members:
        row, col, live = places[m]
        panel = col // 128
        shift = col % 128
        back_shift = (128 - shift) % 128
        keep = lane < 128 - shift

        def cut(part):
            rolled = [
                pltpu.roll(ext_ref[part, panel + i, pl.ds(row, FRAME), :], back_shift, 1)
                for i in range(3)
            ]
            return [jnp.where(keep, rolled[i], rolled[i + 1]) for i in range(2)]

        patch_re = cut(0)
        patch_im = cut(1)
        ex_re, ex_im = [], []
        for h in range(2):
            lanes = slice(128 * h, 128 * h + 128)
            pr = probe_ref[0, :, lanes]
            pi = probe_ref[1, :, lanes]
            ex_re.append(pr * patch_re[h] - pi * patch_im[h])
            ex_im.append(pr * patch_im[h] + pi * patch_re[h])
        xs[0, rows_of(m), 0:128] = (ex_re[0] + ex_re[1]).astype(BF16)
        xs[0, rows_of(m), 128:256] = (ex_im[0] + ex_im[1]).astype(BF16)
        xs[1, rows_of(m), 0:128] = (ex_re[0] - ex_re[1]).astype(BF16)
        xs[1, rows_of(m), 128:256] = (ex_im[0] - ex_im[1]).astype(BF16)
    halves = [dot(xs[q], table_ref[q]) for q in range(2)]
    for m in members:
        for q in range(2):
            half = halves[q][rows_of(m)]
            top, bottom = half[:HALF], half[HALF:]
            lanes = slice(128 * q, 128 * q + 128)
            for p, fold in ((0, top + bottom), (1, top - bottom)):
                folded = fold.astype(BF16)
                gs[m, p, 0:HALF, lanes] = folded[:, :128]
                gs[m, p, HALF:, lanes] = folded[:, 128:]
    for m in members:
        for p in range(2):
            take(m, p, dot(table_ref[2 + p], gs[m, p]))


def update(m, p, far, amp_ref, ds):
    for q in range(2):
        lanes = slice(128 * q, 128 * q + 128)
        far_re, far_im = far[:HALF, lanes], far[HALF:, lanes]
        a = amp_ref[m, FRAME * q + HALF * p : FRAME * q + HALF * p + HALF, :].astype(F32)
        factor = a * lax.rsqrt(far_re * far_re + far_im * far_im + 1.0) - 1.0
        ds[q, rows_of(m, p, HALF), 0:128] = (far_re * factor).astype(BF16)
        ds[q, rows_of(m, p, HALF), 128:256] = (far_im * factor).astype(BF16)


def backward(places, probe_ref, table_ref, acc_ref, ds, ms):
    members = range(len(places))
    lane = lax.broadcasted_iota(jnp.int32, (HALF, 128), 1)
    evens = dot(ds[0], table_ref[4])
    odds = dot(ds[1], table_ref[5])
    for m in members:
        even, odd = evens[rows_of(m)], odds[rows_of(m)]
        for h, mid in ((0, (even + odd).astype(BF16)), (1, (even - odd).astype(BF16))):
            lanes = slice(128 * h, 128 * h + 128)
            for p in range(2):
                rows = slice(HALF * p, HALF * p + HALF)
                ms[m, p, 0:HALF, lanes] = mid[rows, :128]
                ms[m, p, HALF:, lanes] = mid[rows, 128:]
    for m in members:
        row, col, live = places[m]
        shift = col % 128
        panel = jnp.where(live > 0, col // 128, PANELS)
        even = dot(table_ref[6], ms[m, 0])
        odd = dot(table_ref[7], ms[m, 1])
        keep = lane < shift
        for v in range(2):
            back = even + odd if v == 0 else even - odd
            back_re, back_im = back[:HALF], back[HALF:]
            rows = slice(HALF * v, HALF * v + HALF)
            pr = probe_ref[0, rows]
            pi = probe_ref[1, rows]
            where = pl.ds(row + HALF * v, HALF)
            for part, term in ((0, pr * back_re + pi * back_im), (1, pr * back_im - pi * back_re)):
                left = pltpu.roll(term[:, :128], shift, 1)
                right = pltpu.roll(term[:, 128:], shift, 1)
                acc_ref[part, panel, where, :] += jnp.where(keep, 0.0, left)
                acc_ref[part, panel + 1, where, :] += jnp.where(keep, left, right)
                acc_ref[part, panel + 2, where, :] += jnp.where(keep, right, 0.0)


def places_of(meta_ref, rank, group):
    places = [[meta_ref[3 * rank + k, group * GROUP + m] for k in range(3)] for m in range(GROUP)]
    live = places[0][2]
    for place in places[1:]:
        live = live + place[2]
    return places, live > 0


def first_kernel(
    meta_ref, amp_ref, probe_ref, table_ref, ext_ref, out_hbm, far_ref, acc_ref, sems, xs, gs, ds, ms
):
    step = pl.program_id(0)
    groups = pl.num_programs(0) // 2

    def save():
        return pltpu.make_async_copy(acc_ref.at[:, pl.ds(0, PANELS)], out_hbm, sems.at[0])

    @pl.when(step == 0)
    def _():
        acc_ref[:, 0:PANELS] = jnp.zeros_like(ext_ref)
        inner = slice(HALF, HALF + TILE)
        acc_ref[:, 1 : PANELS - 1, inner, :] = 2.0 * ext_ref[:, 1 : PANELS - 1, inner, :]

    places, live = places_of(meta_ref, 0, jnp.minimum(step, groups - 1))

    @pl.when(live & (step < groups))
    def _():
        def take(m, p, far):
            update(m, p, far, amp_ref, ds)

        forward(places, probe_ref, table_ref, ext_ref, xs, gs, take)
        backward(places, probe_ref, table_ref, acc_ref, ds, ms)

    @pl.when(step == groups - 1)
    def _():
        save().start()

    later, live = places_of(meta_ref, 1, jnp.maximum(step - groups, 0))

    @pl.when(live & (step >= groups))
    def _():
        def take(m, p, far):
            far_ref[m, p] = far.astype(BF16)

        forward(later, probe_ref, table_ref, ext_ref, xs, gs, take)

    @pl.when(step == pl.num_programs(0) - 1)
    def _():
        save().wait()


def last_kernel(
    meta_ref, amp_ref, far_ref, probe_ref, table_ref, start_hbm,
    west_ref, east_ref, top_ref, bottom_ref, inner_ref, acc_ref, start_ref, sems, ds, ms,
):
    step = pl.program_id(0)

    def load():
        return pltpu.make_async_copy(start_hbm, start_ref, sems.at[0])

    @pl.when(step == 0)
    def _():
        load().start()
        acc_ref[:, 0:PANELS] = jnp.zeros_like(start_ref)

    places, live = places_of(meta_ref, 1, step)

    @pl.when(live)
    def _():
        for m in range(GROUP):
            for p in range(2):
                update(m, p, far_ref[m, p].astype(F32), amp_ref, ds)
        backward(places, probe_ref, table_ref, acc_ref, ds, ms)

    @pl.when(step == pl.num_programs(0) - 1)
    def _():
        load().wait()

        def half_sum(part, panel, rows):
            return 0.5 * (acc_ref[part, panel, rows, :] + start_ref[part, panel, rows, :])

        for part in range(2):
            west_ref[part] = half_sum(part, 0, slice(0, EXTENT)).astype(BF16)
            east_ref[part] = half_sum(part, PANELS - 1, slice(0, EXTENT)).astype(BF16)
            for j in range(TILE // 128):
                lanes = slice(128 * j, 128 * j + 128)
                top_ref[part, :, lanes] = half_sum(part, j + 1, slice(0, HALF))
                inner_ref[part, :, lanes] = half_sum(part, j + 1, slice(HALF, HALF + TILE))
                bottom_ref[part, :, lanes] = half_sum(part, j + 1, slice(HALF + TILE, EXTENT))


def whole(shape):
    return pl.BlockSpec(shape, lambda s, m: (0,) * len(shape))


WIDE = (2, PANELS, EXTENT, 128)
SUMS = (2, PANELS + 3, EXTENT, 128)
FLAT = (2, GROUP * FRAME, FRAME)
DEEP = (GROUP, 2, FRAME, FRAME)


def run_first(meta, amps, probe, tabs, ext):
    groups = amps.shape[0] // GROUP
    return pl.pallas_call(
        first_kernel,
        grid_spec=pltpu.PrefetchScalarGridSpec(
            num_scalar_prefetch=1,
            grid=(2 * groups,),
            in_specs=[
                pl.BlockSpec(
                    (GROUP,) + amps.shape[1:], lambda s, m: (jnp.minimum(s, groups - 1), 0, 0)
                ),
                whole((2, FRAME, FRAME)),
                whole((8, FRAME, FRAME)),
                whole(WIDE),
            ],
            out_specs=[
                pl.BlockSpec(memory_space=pl.ANY),
                pl.BlockSpec(DEEP, lambda s, m: (jnp.maximum(s - groups, 0), 0, 0, 0)),
            ],
            scratch_shapes=[pltpu.VMEM(SUMS, F32), pltpu.SemaphoreType.DMA((1,))]
            + [pltpu.VMEM(shape, BF16) for shape in (FLAT, DEEP, FLAT, DEEP)],
        ),
        out_shape=[
            jax.ShapeDtypeStruct(WIDE, F32),
            jax.ShapeDtypeStruct((amps.shape[0], 2, FRAME, FRAME), BF16),
        ],
        compiler_params=pltpu.CompilerParams(vmem_limit_bytes=34 << 20),
        cost_estimate=pl.CostEstimate(
            flops=2 * amps.shape[0] * 16 * FRAME**3, bytes_accessed=24 << 20, transcendentals=0
        ),
        name="first",
    )(meta, amps, probe, tabs, ext)


def run_last(meta, amps, far, probe, tabs, start):
    groups = amps.shape[0] // GROUP
    shapes = [(2, EXTENT, 128)] * 2 + [(2, HALF, TILE)] * 2 + [(2, TILE, TILE)]
    return pl.pallas_call(
        last_kernel,
        grid_spec=pltpu.PrefetchScalarGridSpec(
            num_scalar_prefetch=1,
            grid=(groups,),
            in_specs=[
                pl.BlockSpec((GROUP,) + amps.shape[1:], lambda s, m: (s, 0, 0)),
                pl.BlockSpec(DEEP, lambda s, m: (s, 0, 0, 0)),
                whole((2, FRAME, FRAME)),
                whole((8, FRAME, FRAME)),
                pl.BlockSpec(memory_space=pl.ANY),
            ],
            out_specs=[whole(shape) for shape in shapes],
            scratch_shapes=[
                pltpu.VMEM(SUMS, F32),
                pltpu.VMEM(WIDE, F32),
                pltpu.SemaphoreType.DMA((1,)),
                pltpu.VMEM(FLAT, BF16),
                pltpu.VMEM(DEEP, BF16),
            ],
        ),
        out_shape=[jax.ShapeDtypeStruct(s, d) for s, d in zip(shapes, (BF16, BF16, F32, F32, F32))],
        compiler_params=pltpu.CompilerParams(vmem_limit_bytes=34 << 20),
        cost_estimate=pl.CostEstimate(
            flops=amps.shape[0] * 8 * FRAME**3, bytes_accessed=20 << 20, transcendentals=0
        ),
        name="last",
    )(meta, amps, far, probe, tabs, start)


def across_kernel(top_ref, bottom_ref, west_n, west_s, east_n, east_s, north_ref, south_ref):
    for base, west, east, out in (
        (top_ref, west_n, east_n, north_ref), (bottom_ref, west_s, east_s, south_ref)
    ):
        out[:, :, 0:HALF] = (base[:, :, 0:HALF] + west[...].astype(F32)).astype(BF16)
        out[:, :, HALF : TILE - HALF] = base[:, :, HALF : TILE - HALF].astype(BF16)
        out[:, :, TILE - HALF :] = (base[:, :, TILE - HALF :] + east[...].astype(F32)).astype(BF16)


def across(top, bottom, from_west, from_east):
    end = EXTENT // HALF - 1
    full = pl.BlockSpec((2, HALF, TILE), lambda i: (0, 0, 0))
    first = pl.BlockSpec((2, HALF, 128), lambda i: (0, 0, 0))
    last = pl.BlockSpec((2, HALF, 128), lambda i: (0, end, 0))
    return pl.pallas_call(
        across_kernel,
        grid=(1,),
        in_specs=[full, full, first, last, first, last],
        out_specs=[full, full],
        out_shape=[jax.ShapeDtypeStruct((2, HALF, TILE), BF16)] * 2,
        compiler_params=pltpu.CompilerParams(vmem_limit_bytes=10 << 20),
        name="across",
    )(top, bottom, from_west, from_west, from_east, from_east)


def sides_kernel(base_ref, west_ref, east_ref, out_ref):
    inner = slice(HALF, HALF + TILE)

    @pl.when(pl.program_id(0) == 0)
    def _():
        out_ref[...] = base_ref[...] + west_ref[:, inner, :].astype(F32)

    @pl.when(pl.program_id(0) == 1)
    def _():
        out_ref[...] = base_ref[...] + east_ref[:, inner, :].astype(F32)


def ends_kernel(base_ref, north_ref, south_ref, out_ref):
    @pl.when(pl.program_id(0) == 0)
    def _():
        out_ref[...] = base_ref[...] + north_ref[...].astype(F32)

    @pl.when(pl.program_id(0) == 1)
    def _():
        out_ref[...] = base_ref[...] + south_ref[...].astype(F32)


def add_pair(kernel, base, block, place, low, high):
    strip = pl.BlockSpec(low.shape, lambda i: (0, 0, 0))
    return pl.pallas_call(
        kernel,
        grid=(2,),
        in_specs=[pl.BlockSpec(block, place), strip, strip],
        out_specs=pl.BlockSpec(block, place),
        out_shape=jax.ShapeDtypeStruct(base.shape, F32),
        input_output_aliases={0: 0},
        compiler_params=pltpu.CompilerParams(vmem_limit_bytes=10 << 20),
        name="ends",
    )(base, low, high)


def shifted(value, axis, by):
    size = lax.axis_size(axis)
    pairs = [(i, i + by) for i in range(size) if 0 <= i + by < size]
    return lax.ppermute(value, axis, pairs)


def body(obj, probe, intensity, dest, offsets):
    groups = lax.axis_size("gx")
    sends = prep(jnp.concatenate([dest.T, offsets.T]).reshape(-1), intensity, groups)
    north = shifted(obj[:, TILE - HALF :, :].astype(BF16), "gy", 1)
    south = shifted(obj[:, :HALF, :].astype(BF16), "gy", -1)
    routed = functools.partial(
        lax.all_to_all, axis_name="gx", split_axis=0, concat_axis=0, tiled=True
    )
    first, north, south = lax.optimization_barrier((sends[0], north, south))
    amps = routed(first)

    def column(lo, hi):
        own = obj[:, :, lo:hi].astype(BF16)
        return jnp.concatenate([north[:, :, lo:hi], own, south[:, :, lo:hi]], axis=1)

    west = shifted(column(TILE - HALF, TILE), "gx", 1)
    east = shifted(column(0, HALF), "gx", -1)
    west, east, rest = lax.optimization_barrier((west, east, sends[1]))
    more = routed(rest)
    ext = assemble(obj, north, south, west, east)
    tabs = jnp.asarray(table_blocks())
    notes = amps[:, 2 * FRAME, :10].astype(jnp.int32).T
    meta = jnp.stack(
        [
            notes[5 * r] * 16 + notes[5 * r + 1] if k == 0 else
            notes[5 * r + 2] * 16 + notes[5 * r + 3] if k == 1 else notes[5 * r + 4]
            for r in range(CAP) for k in range(3)
        ]
    )
    acc, far = run_first(meta, amps, probe, tabs, ext)
    west, east, top, bottom, inner = run_last(meta, more, far, probe, tabs, acc)
    from_west = shifted(east, "gx", 1)
    from_east = shifted(west, "gx", -1)
    to_north, to_south = across(top, bottom, from_west, from_east)
    from_north = shifted(to_south, "gy", 1)
    from_south = shifted(to_north, "gy", -1)
    steps = TILE // HALF - 1
    inner = add_pair(
        sides_kernel, inner, (2, TILE, HALF), lambda i: (0, 0, steps * i), from_west, from_east
    )
    return add_pair(
        ends_kernel, inner, (2, HALF, TILE), lambda i: (0, steps * i, 0), from_north, from_south
    )


def solution(mesh):
    placed = (
        P(None, "gy", "gx"),
        P(),
        P(("gx", "gy"), None, None),
        P(("gx", "gy"), None),
        P(("gx", "gy"), None),
    )
    return jax.shard_map(
        body, mesh=mesh, in_specs=placed, out_specs=P(None, "gy", "gx"), check_vma=False
    )
```

```python
import functools
import math

import jax
import jax.numpy as jnp
import numpy as np
from jax import lax
from jax.experimental import pallas as pl
from jax.experimental.pallas import tpu as pltpu
from jax.sharding import PartitionSpec as P

CAP = 2
FRAME = 256
HALF = 128
TILE = 512
EXTENT = TILE + 2 * HALF
PANELS = EXTENT // 128
NOTE_ROWS = 16
GROUP = 4
BF16 = jnp.bfloat16
F32 = jnp.float32


def table_blocks():
    index = np.arange(FRAME)[:, None] * np.arange(FRAME)[None, :] % FRAME
    angle = index.astype(np.float32) * np.float32(2.0 * math.pi / FRAME)
    scale = np.float32(1.0 / math.sqrt(FRAME))
    re = (np.cos(angle) * scale).astype(BF16)
    im = (-np.sin(angle) * scale).astype(BF16)
    blocks = []
    for parity in (0, 1):
        c = re[:HALF, parity::2]
        s = im[:HALF, parity::2]
        fwd_right = np.block([[c, s], [-s, c]])
        fwd_left = fwd_right.T
        inv_right = np.block([[c.T, -s.T], [s.T, c.T]])
        inv_left = inv_right.T
        blocks.append([fwd_right, fwd_left, inv_right, inv_left])
    return np.stack([blocks[p][i] for i in range(4) for p in (0, 1)]).astype(BF16)


def deinterleave():
    perm = np.zeros((FRAME, FRAME), np.float32)
    for j in range(HALF):
        perm[2 * j, j] = 1.0
        perm[2 * j + 1, HALF + j] = 1.0
    return perm.astype(BF16)


def dot(a, b):
    return jnp.dot(a, b, preferred_element_type=F32)


def prep_kernel(
    where_ref, inten_ref, perm_ref, first_ref, second_ref, stage, split, notes, ranks, sems
):
    step = pl.program_id(0)
    count = pl.num_programs(0)
    per = inten_ref.shape[0]
    groups = first_ref.shape[0]
    slot = step % 2

    def notes_copy():
        return pltpu.make_async_copy(
            notes, first_ref.at[:, pl.ds(2 * FRAME, NOTE_ROWS), :], sems.at[2 * per]
        )

    @pl.when(step == 0)
    def _():
        lane = lax.broadcasted_iota(jnp.int32, (groups, 128), 1)
        owner = lax.broadcasted_iota(jnp.int32, (groups, 128), 0)
        note = jnp.zeros((groups, 128), jnp.int32)
        for g in range(groups):
            ranks[per * count + g] = 0
        for f in range(per * count):
            mine = where_ref[f]
            rank = ranks[per * count + mine]
            ranks[f] = rank
            ranks[per * count + mine] = rank + 1
            row, col = where_ref[per * count + f], where_ref[2 * per * count + f]
            at = lane - 5 * rank
            value = jnp.where(at == 0, row // 16, jnp.where(at == 1, row % 16, 0))
            value += jnp.where(at == 2, col // 16, jnp.where(at == 3, col % 16, 0))
            value += jnp.where(at == 4, 1, 0)
            note = jnp.where(owner == mine, note + value, note)
        notes[...] = jnp.broadcast_to(note.astype(F32)[:, None, :], notes.shape).astype(BF16)
        notes_copy().start()

    for i in range(per):

        @pl.when(step >= 2)
        def _():
            pltpu.make_async_copy(
                stage.at[slot, i], second_ref.at[0], sems.at[slot * per + i]
            ).wait()

    for i in range(per):
        for h in range(2):
            split[i, h] = jnp.sqrt(inten_ref[i, :, 128 * h : 128 * h + 128])
        rows = [
            jnp.concatenate([split[i, h, pl.ds(p, HALF, 2), :] for h in range(2)], axis=1)
            for p in range(2)
        ]
        amp = jnp.concatenate(rows, axis=0).astype(BF16)
        cols = dot(amp, perm_ref[...]).astype(BF16)
        stage[slot, i, 0:FRAME, :] = cols[:, :128]
        stage[slot, i, FRAME : 2 * FRAME, :] = cols[:, 128:]
    for i in range(per):
        f = step * per + i
        mine = where_ref[f]
        rank = ranks[f]

        @pl.when(rank == 0)
        def _():
            pltpu.make_async_copy(
                stage.at[slot, i],
                first_ref.at[mine, pl.ds(0, 2 * FRAME), :],
                sems.at[slot * per + i],
            ).start()

        @pl.when(rank != 0)
        def _():
            pltpu.make_async_copy(
                stage.at[slot, i], second_ref.at[mine], sems.at[slot * per + i]
            ).start()

    @pl.when(step == count - 1)
    def _():
        notes_copy().wait()
        for s in range(2):
            for i in range(per):
                pltpu.make_async_copy(
                    stage.at[s, i], second_ref.at[0], sems.at[s * per + i]
                ).wait()


def prep(where, intensity, groups):
    frames = intensity.shape[0]
    per = 4
    return pl.pallas_call(
        prep_kernel,
        grid_spec=pltpu.PrefetchScalarGridSpec(
            num_scalar_prefetch=1,
            grid=(frames // per,),
            in_specs=[
                pl.BlockSpec((per, FRAME, FRAME), lambda s, w: (s, 0, 0)),
                pl.BlockSpec((FRAME, FRAME), lambda s, w: (0, 0)),
            ],
            out_specs=[pl.BlockSpec(memory_space=pl.ANY)] * 2,
            scratch_shapes=[
                pltpu.VMEM((2, per, 2 * FRAME, 128), BF16),
                pltpu.VMEM((per, 2, FRAME, 128), F32),
                pltpu.VMEM((groups, NOTE_ROWS, 128), BF16),
                pltpu.SMEM((frames + groups,), jnp.int32),
                pltpu.SemaphoreType.DMA((2 * per + 1,)),
            ],
        ),
        out_shape=[
            jax.ShapeDtypeStruct((groups, 2 * FRAME + NOTE_ROWS, 128), BF16),
            jax.ShapeDtypeStruct((groups, 2 * FRAME, 128), BF16),
        ],
        compiler_params=pltpu.CompilerParams(vmem_limit_bytes=56 << 20),
        cost_estimate=pl.CostEstimate(
            flops=frames * 2 * FRAME**3, bytes_accessed=frames * FRAME * FRAME * 6, transcendentals=0
        ),
        name="prep",
    )(where, intensity, jnp.asarray(deinterleave()))


def tile_copies(obj_hbm, ext_ref, sems):
    return [
        pltpu.make_async_copy(
            obj_hbm.at[part, :, pl.ds(128 * j, 128)],
            ext_ref.at[part, j + 1, pl.ds(HALF, TILE), :],
            sems.at[1 + part * (TILE // 128) + j],
        )
        for part in range(2)
        for j in range(TILE // 128)
    ]


def set_halo(north_ref, south_ref, west_ref, east_ref, ext_ref):
    for part in range(2):
        ext_ref[part, 0] = west_ref[part].astype(F32)
        ext_ref[part, PANELS - 1] = east_ref[part].astype(F32)
        for j in range(TILE // 128):
            lanes = slice(128 * j, 128 * j + 128)
            ext_ref[part, j + 1, 0:HALF, :] = north_ref[part, :, lanes].astype(F32)
            ext_ref[part, j + 1, HALF + TILE :, :] = south_ref[part, :, lanes].astype(F32)


def rows_of(m, p=0, height=FRAME):
    return slice(FRAME * m + HALF * p, FRAME * m + HALF * p + height)


def forward(places, probe_ref, table_ref, ext_ref, xs, gs, take):
    members = range(len(places))
    lane = lax.broadcasted_iota(jnp.int32, (FRAME, 128), 1)
    for m in members:
        row, col, live = places[m]
        panel = col // 128
        shift = col % 128
        back_shift = (128 - shift) % 128
        keep = lane < 128 - shift

        def cut(part):
            rolled = [
                pltpu.roll(ext_ref[part, panel + i, pl.ds(row, FRAME), :], back_shift, 1)
                for i in range(3)
            ]
            return [jnp.where(keep, rolled[i], rolled[i + 1]) for i in range(2)]

        patch_re = cut(0)
        patch_im = cut(1)
        ex_re, ex_im = [], []
        for h in range(2):
            lanes = slice(128 * h, 128 * h + 128)
            pr = probe_ref[0, :, lanes]
            pi = probe_ref[1, :, lanes]
            ex_re.append(pr * patch_re[h] - pi * patch_im[h])
            ex_im.append(pr * patch_im[h] + pi * patch_re[h])
        xs[0, rows_of(m), 0:128] = (ex_re[0] + ex_re[1]).astype(BF16)
        xs[0, rows_of(m), 128:256] = (ex_im[0] + ex_im[1]).astype(BF16)
        xs[1, rows_of(m), 0:128] = (ex_re[0] - ex_re[1]).astype(BF16)
        xs[1, rows_of(m), 128:256] = (ex_im[0] - ex_im[1]).astype(BF16)
    halves = [dot(xs[q], table_ref[q]) for q in range(2)]
    for m in members:
        for q in range(2):
            half = halves[q][rows_of(m)]
            top, bottom = half[:HALF], half[HALF:]
            lanes = slice(128 * q, 128 * q + 128)
            for p, fold in ((0, top + bottom), (1, top - bottom)):
                folded = fold.astype(BF16)
                gs[m, p, 0:HALF, lanes] = folded[:, :128]
                gs[m, p, HALF:, lanes] = folded[:, 128:]
    for m in members:
        for p in range(2):
            take(m, p, dot(table_ref[2 + p], gs[m, p]))


def update(m, p, far, amp_ref, ds):
    for q in range(2):
        lanes = slice(128 * q, 128 * q + 128)
        far_re, far_im = far[:HALF, lanes], far[HALF:, lanes]
        a = amp_ref[m, FRAME * q + HALF * p : FRAME * q + HALF * p + HALF, :].astype(F32)
        factor = a * lax.rsqrt(far_re * far_re + far_im * far_im + 1.0) - 1.0
        ds[q, rows_of(m, p, HALF), 0:128] = (far_re * factor).astype(BF16)
        ds[q, rows_of(m, p, HALF), 128:256] = (far_im * factor).astype(BF16)


def backward(places, probe_ref, table_ref, acc_ref, ds, ms):
    members = range(len(places))
    lane = lax.broadcasted_iota(jnp.int32, (HALF, 128), 1)
    evens = dot(ds[0], table_ref[4])
    odds = dot(ds[1], table_ref[5])
    for m in members:
        even, odd = evens[rows_of(m)], odds[rows_of(m)]
        for h, mid in ((0, (even + odd).astype(BF16)), (1, (even - odd).astype(BF16))):
            lanes = slice(128 * h, 128 * h + 128)
            for p in range(2):
                rows = slice(HALF * p, HALF * p + HALF)
                ms[m, p, 0:HALF, lanes] = mid[rows, :128]
                ms[m, p, HALF:, lanes] = mid[rows, 128:]
    for m in members:
        row, col, live = places[m]
        shift = col % 128
        panel = jnp.where(live > 0, col // 128, PANELS)
        even = dot(table_ref[6], ms[m, 0])
        odd = dot(table_ref[7], ms[m, 1])
        keep = lane < shift
        for v in range(2):
            back = even + odd if v == 0 else even - odd
            back_re, back_im = back[:HALF], back[HALF:]
            rows = slice(HALF * v, HALF * v + HALF)
            pr = probe_ref[0, rows]
            pi = probe_ref[1, rows]
            where = pl.ds(row + HALF * v, HALF)
            for part, term in ((0, pr * back_re + pi * back_im), (1, pr * back_im - pi * back_re)):
                left = pltpu.roll(term[:, :128], shift, 1)
                right = pltpu.roll(term[:, 128:], shift, 1)
                acc_ref[part, panel, where, :] += jnp.where(keep, 0.0, left)
                acc_ref[part, panel + 1, where, :] += jnp.where(keep, left, right)
                acc_ref[part, panel + 2, where, :] += jnp.where(keep, right, 0.0)


def places_of(meta_ref, rank, group):
    places = [[meta_ref[3 * rank + k, group * GROUP + m] for k in range(3)] for m in range(GROUP)]
    live = places[0][2]
    for place in places[1:]:
        live = live + place[2]
    return places, live > 0


def first_kernel(
    meta_ref, amp_ref, probe_ref, table_ref, north_ref, south_ref, west_ref, east_ref, obj_hbm,
    out_hbm, far_ref, ext_ref, acc_ref, sems, xs, gs, ds, ms,
):
    step = pl.program_id(0)
    groups = pl.num_programs(0) // 2

    def save():
        return pltpu.make_async_copy(acc_ref.at[:, pl.ds(0, PANELS)], out_hbm, sems.at[0])

    @pl.when(step == 0)
    def _():
        copies = tile_copies(obj_hbm, ext_ref, sems)
        for copy in copies:
            copy.start()
        acc_ref[:, 0:PANELS] = jnp.zeros_like(ext_ref)
        set_halo(north_ref, south_ref, west_ref, east_ref, ext_ref)
        for copy in copies:
            copy.wait()
        inner = slice(HALF, HALF + TILE)
        acc_ref[:, 1 : PANELS - 1, inner, :] = 2.0 * ext_ref[:, 1 : PANELS - 1, inner, :]

    places, live = places_of(meta_ref, 0, jnp.minimum(step, groups - 1))

    @pl.when(live & (step < groups))
    def _():
        def take(m, p, far):
            update(m, p, far, amp_ref, ds)

        forward(places, probe_ref, table_ref, ext_ref, xs, gs, take)
        backward(places, probe_ref, table_ref, acc_ref, ds, ms)

    @pl.when(step == groups - 1)
    def _():
        save().start()

    later, live = places_of(meta_ref, 1, jnp.maximum(step - groups, 0))

    @pl.when(live & (step >= groups))
    def _():
        def take(m, p, far):
            far_ref[m, p] = far.astype(BF16)

        forward(later, probe_ref, table_ref, ext_ref, xs, gs, take)

    @pl.when(step == pl.num_programs(0) - 1)
    def _():
        save().wait()


def last_kernel(
    meta_ref, amp_ref, far_ref, probe_ref, table_ref, start_hbm,
    west_ref, east_ref, top_ref, bottom_ref, inner_ref, acc_ref, start_ref, sems, ds, ms,
):
    step = pl.program_id(0)

    def load():
        return pltpu.make_async_copy(start_hbm, start_ref, sems.at[0])

    @pl.when(step == 0)
    def _():
        load().start()
        acc_ref[:, 0:PANELS] = jnp.zeros_like(start_ref)

    places, live = places_of(meta_ref, 1, step)

    @pl.when(live)
    def _():
        for m in range(GROUP):
            for p in range(2):
                update(m, p, far_ref[m, p].astype(F32), amp_ref, ds)
        backward(places, probe_ref, table_ref, acc_ref, ds, ms)

    @pl.when(step == pl.num_programs(0) - 1)
    def _():
        load().wait()

        def half_sum(part, panel, rows):
            return 0.5 * (acc_ref[part, panel, rows, :] + start_ref[part, panel, rows, :])

        for part in range(2):
            west_ref[part] = half_sum(part, 0, slice(0, EXTENT)).astype(BF16)
            east_ref[part] = half_sum(part, PANELS - 1, slice(0, EXTENT)).astype(BF16)
            for j in range(TILE // 128):
                lanes = slice(128 * j, 128 * j + 128)
                top_ref[part, :, lanes] = half_sum(part, j + 1, slice(0, HALF))
                inner_ref[part, :, lanes] = half_sum(part, j + 1, slice(HALF, HALF + TILE))
                bottom_ref[part, :, lanes] = half_sum(part, j + 1, slice(HALF + TILE, EXTENT))


def whole(shape):
    return pl.BlockSpec(shape, lambda s, m: (0,) * len(shape))


WIDE = (2, PANELS, EXTENT, 128)
SUMS = (2, PANELS + 3, EXTENT, 128)
FLAT = (2, GROUP * FRAME, FRAME)
DEEP = (GROUP, 2, FRAME, FRAME)


def run_first(meta, amps, probe, tabs, obj, north, south, west, east):
    groups = amps.shape[0] // GROUP
    return pl.pallas_call(
        first_kernel,
        grid_spec=pltpu.PrefetchScalarGridSpec(
            num_scalar_prefetch=1,
            grid=(2 * groups,),
            in_specs=[
                pl.BlockSpec(
                    (GROUP,) + amps.shape[1:], lambda s, m: (jnp.minimum(s, groups - 1), 0, 0)
                ),
                whole((2, FRAME, FRAME)),
                whole((8, FRAME, FRAME)),
                whole(north.shape),
                whole(south.shape),
                whole(west.shape),
                whole(east.shape),
                pl.BlockSpec(memory_space=pl.ANY),
            ],
            out_specs=[
                pl.BlockSpec(memory_space=pl.ANY),
                pl.BlockSpec(DEEP, lambda s, m: (jnp.maximum(s - groups, 0), 0, 0, 0)),
            ],
            scratch_shapes=[
                pltpu.VMEM(WIDE, F32),
                pltpu.VMEM(SUMS, F32),
                pltpu.SemaphoreType.DMA((1 + 2 * TILE // 128,)),
            ]
            + [pltpu.VMEM(shape, BF16) for shape in (FLAT, DEEP, FLAT, DEEP)],
        ),
        out_shape=[
            jax.ShapeDtypeStruct(WIDE, F32),
            jax.ShapeDtypeStruct((amps.shape[0], 2, FRAME, FRAME), BF16),
        ],
        compiler_params=pltpu.CompilerParams(vmem_limit_bytes=56 << 20),
        cost_estimate=pl.CostEstimate(
            flops=2 * amps.shape[0] * 16 * FRAME**3, bytes_accessed=24 << 20, transcendentals=0
        ),
        name="first",
    )(meta, amps, probe, tabs, north, south, west, east, obj)


def run_last(meta, amps, far, probe, tabs, start):
    groups = amps.shape[0] // GROUP

    def used(s, m):
        live = m[5, s * GROUP]
        for k in range(1, GROUP):
            live = live + m[5, s * GROUP + k]
        return jnp.where(live > 0, s, 0)

    shapes = [(2, EXTENT, 128)] * 2 + [(2, HALF, TILE)] * 2 + [(2, TILE, TILE)]
    return pl.pallas_call(
        last_kernel,
        grid_spec=pltpu.PrefetchScalarGridSpec(
            num_scalar_prefetch=1,
            grid=(groups,),
            in_specs=[
                pl.BlockSpec((GROUP,) + amps.shape[1:], lambda s, m: (used(s, m), 0, 0)),
                pl.BlockSpec(DEEP, lambda s, m: (used(s, m), 0, 0, 0)),
                whole((2, FRAME, FRAME)),
                whole((8, FRAME, FRAME)),
                pl.BlockSpec(memory_space=pl.ANY),
            ],
            out_specs=[whole(shape) for shape in shapes],
            scratch_shapes=[
                pltpu.VMEM(SUMS, F32),
                pltpu.VMEM(WIDE, F32),
                pltpu.SemaphoreType.DMA((1,)),
                pltpu.VMEM(FLAT, BF16),
                pltpu.VMEM(DEEP, BF16),
            ],
        ),
        out_shape=[jax.ShapeDtypeStruct(s, d) for s, d in zip(shapes, (BF16, BF16, F32, F32, F32))],
        compiler_params=pltpu.CompilerParams(vmem_limit_bytes=56 << 20),
        cost_estimate=pl.CostEstimate(
            flops=amps.shape[0] * 8 * FRAME**3, bytes_accessed=20 << 20, transcendentals=0
        ),
        name="last",
    )(meta, amps, far, probe, tabs, start)


def across_kernel(top_ref, bottom_ref, west_n, west_s, east_n, east_s, north_ref, south_ref):
    for base, west, east, out in (
        (top_ref, west_n, east_n, north_ref), (bottom_ref, west_s, east_s, south_ref)
    ):
        out[:, :, 0:HALF] = (base[:, :, 0:HALF] + west[...].astype(F32)).astype(BF16)
        out[:, :, HALF : TILE - HALF] = base[:, :, HALF : TILE - HALF].astype(BF16)
        out[:, :, TILE - HALF :] = (base[:, :, TILE - HALF :] + east[...].astype(F32)).astype(BF16)


def across(top, bottom, from_west, from_east):
    end = EXTENT // HALF - 1
    full = pl.BlockSpec((2, HALF, TILE), lambda i: (0, 0, 0))
    first = pl.BlockSpec((2, HALF, 128), lambda i: (0, 0, 0))
    last = pl.BlockSpec((2, HALF, 128), lambda i: (0, end, 0))
    return pl.pallas_call(
        across_kernel,
        grid=(1,),
        in_specs=[full, full, first, last, first, last],
        out_specs=[full, full],
        out_shape=[jax.ShapeDtypeStruct((2, HALF, TILE), BF16)] * 2,
        compiler_params=pltpu.CompilerParams(vmem_limit_bytes=10 << 20),
        name="across",
    )(top, bottom, from_west, from_west, from_east, from_east)


def sides_kernel(base_ref, west_ref, east_ref, out_ref):
    inner = slice(HALF, HALF + TILE)

    @pl.when(pl.program_id(0) == 0)
    def _():
        out_ref[...] = base_ref[...] + west_ref[:, inner, :].astype(F32)

    @pl.when(pl.program_id(0) == 1)
    def _():
        out_ref[...] = base_ref[...] + east_ref[:, inner, :].astype(F32)


def ends_kernel(base_ref, north_ref, south_ref, out_ref):
    @pl.when(pl.program_id(0) == 0)
    def _():
        out_ref[...] = base_ref[...] + north_ref[...].astype(F32)

    @pl.when(pl.program_id(0) == 1)
    def _():
        out_ref[...] = base_ref[...] + south_ref[...].astype(F32)


def add_pair(kernel, base, block, place, low, high):
    strip = pl.BlockSpec(low.shape, lambda i: (0, 0, 0))
    return pl.pallas_call(
        kernel,
        grid=(2,),
        in_specs=[pl.BlockSpec(block, place), strip, strip],
        out_specs=pl.BlockSpec(block, place),
        out_shape=jax.ShapeDtypeStruct(base.shape, F32),
        input_output_aliases={0: 0},
        compiler_params=pltpu.CompilerParams(vmem_limit_bytes=10 << 20),
        name="ends",
    )(base, low, high)


def shifted(value, axis, by):
    size = lax.axis_size(axis)
    pairs = [(i, i + by) for i in range(size) if 0 <= i + by < size]
    return lax.ppermute(value, axis, pairs)


def body(obj, probe, intensity, dest, offsets):
    groups = lax.axis_size("gx")
    sends = prep(jnp.concatenate([dest.T, offsets.T]).reshape(-1), intensity, groups)
    north = shifted(obj[:, TILE - HALF :, :].astype(BF16), "gy", 1)
    south = shifted(obj[:, :HALF, :].astype(BF16), "gy", -1)
    routed = functools.partial(
        lax.all_to_all, axis_name="gx", split_axis=0, concat_axis=0, tiled=True
    )
    first, north, south = lax.optimization_barrier((sends[0], north, south))
    amps = routed(first)

    def column(lo, hi):
        own = obj[:, :, lo:hi].astype(BF16)
        return jnp.concatenate([north[:, :, lo:hi], own, south[:, :, lo:hi]], axis=1)

    west = shifted(column(TILE - HALF, TILE), "gx", 1)
    east = shifted(column(0, HALF), "gx", -1)
    west, east, rest = lax.optimization_barrier((west, east, sends[1]))
    more = routed(rest)
    tabs = jnp.asarray(table_blocks())
    notes = amps[:, 2 * FRAME, :10].astype(jnp.int32).T
    meta = jnp.stack(
        [
            notes[5 * r] * 16 + notes[5 * r + 1] if k == 0 else
            notes[5 * r + 2] * 16 + notes[5 * r + 3] if k == 1 else notes[5 * r + 4]
            for r in range(CAP) for k in range(3)
        ]
    )
    acc, far = run_first(meta, amps, probe, tabs, obj, north, south, west, east)
    west, east, top, bottom, inner = run_last(meta, more, far, probe, tabs, acc)
    from_west = shifted(east, "gx", 1)
    from_east = shifted(west, "gx", -1)
    to_north, to_south = across(top, bottom, from_west, from_east)
    from_north = shifted(to_south, "gy", 1)
    from_south = shifted(to_north, "gy", -1)
    steps = TILE // HALF - 1
    inner = add_pair(
        sides_kernel, inner, (2, TILE, HALF), lambda i: (0, 0, steps * i), from_west, from_east
    )
    return add_pair(
        ends_kernel, inner, (2, HALF, TILE), lambda i: (0, steps * i, 0), from_north, from_south
    )


def solution(mesh):
    placed = (
        P(None, "gy", "gx"),
        P(),
        P(("gx", "gy"), None, None),
        P(("gx", "gy"), None),
        P(("gx", "gy"), None),
    )
    return jax.shard_map(
        body, mesh=mesh, in_specs=placed, out_specs=P(None, "gy", "gx"), check_vma=False
    )
```

```python
import functools
import math

import jax
import jax.numpy as jnp
import numpy as np
from jax import lax
from jax.experimental import pallas as pl
from jax.experimental.pallas import tpu as pltpu
from jax.sharding import PartitionSpec as P

CAP = 2
FRAME = 256
HALF = 128
TILE = 512
EXTENT = TILE + 2 * HALF
PANELS = EXTENT // 128
NOTE_ROWS = 16
GROUP = 4
BF16 = jnp.bfloat16
F32 = jnp.float32


def table_blocks():
    index = np.arange(FRAME)[:, None] * np.arange(FRAME)[None, :] % FRAME
    angle = index.astype(np.float32) * np.float32(2.0 * math.pi / FRAME)
    scale = np.float32(1.0 / math.sqrt(FRAME))
    re = (np.cos(angle) * scale).astype(BF16)
    im = (-np.sin(angle) * scale).astype(BF16)
    blocks = []
    for parity in (0, 1):
        c = re[:HALF, parity::2]
        s = im[:HALF, parity::2]
        fwd_right = np.block([[c, s], [-s, c]])
        fwd_left = fwd_right.T
        inv_right = np.block([[c.T, -s.T], [s.T, c.T]])
        inv_left = inv_right.T
        blocks.append([fwd_right, fwd_left, inv_right, inv_left])
    return np.stack([blocks[p][i] for i in range(4) for p in (0, 1)]).astype(BF16)


def deinterleave():
    perm = np.zeros((FRAME, FRAME), np.float32)
    for j in range(HALF):
        perm[2 * j, j] = 1.0
        perm[2 * j + 1, HALF + j] = 1.0
    return perm.astype(BF16)


def dot(a, b):
    return jnp.dot(a, b, preferred_element_type=F32)


def prep_kernel(
    where_ref, inten_ref, perm_ref, first_ref, second_ref, stage, split, notes, ranks, sems
):
    step = pl.program_id(0)
    count = pl.num_programs(0)
    per = inten_ref.shape[0]
    groups = first_ref.shape[0]
    slot = step % 2

    def notes_copy():
        return pltpu.make_async_copy(
            notes, first_ref.at[:, pl.ds(2 * FRAME, NOTE_ROWS), :], sems.at[2 * per]
        )

    @pl.when(step == 0)
    def _():
        lane = lax.broadcasted_iota(jnp.int32, (groups, 128), 1)
        owner = lax.broadcasted_iota(jnp.int32, (groups, 128), 0)
        note = jnp.zeros((groups, 128), jnp.int32)
        for g in range(groups):
            ranks[per * count + g] = 0
        for f in range(per * count):
            mine = where_ref[f]
            rank = ranks[per * count + mine]
            ranks[f] = rank
            ranks[per * count + mine] = rank + 1
            row, col = where_ref[per * count + f], where_ref[2 * per * count + f]
            at = lane - 5 * rank
            value = jnp.where(at == 0, row // 16, jnp.where(at == 1, row % 16, 0))
            value += jnp.where(at == 2, col // 16, jnp.where(at == 3, col % 16, 0))
            value += jnp.where(at == 4, 1, 0)
            note = jnp.where(owner == mine, note + value, note)
        notes[...] = jnp.broadcast_to(note.astype(F32)[:, None, :], notes.shape).astype(BF16)
        notes_copy().start()

    for i in range(per):

        @pl.when(step >= 2)
        def _():
            pltpu.make_async_copy(
                stage.at[slot, i], second_ref.at[0], sems.at[slot * per + i]
            ).wait()

    for i in range(per):
        for h in range(2):
            split[i, h] = jnp.sqrt(inten_ref[i, :, 128 * h : 128 * h + 128])
        rows = [
            jnp.concatenate([split[i, h, pl.ds(p, HALF, 2), :] for h in range(2)], axis=1)
            for p in range(2)
        ]
        amp = jnp.concatenate(rows, axis=0).astype(BF16)
        cols = dot(amp, perm_ref[...]).astype(BF16)
        stage[slot, i, 0:FRAME, :] = cols[:, :128]
        stage[slot, i, FRAME : 2 * FRAME, :] = cols[:, 128:]
    for i in range(per):
        f = step * per + i
        mine = where_ref[f]
        rank = ranks[f]

        @pl.when(rank == 0)
        def _():
            pltpu.make_async_copy(
                stage.at[slot, i],
                first_ref.at[mine, pl.ds(0, 2 * FRAME), :],
                sems.at[slot * per + i],
            ).start()

        @pl.when(rank != 0)
        def _():
            pltpu.make_async_copy(
                stage.at[slot, i], second_ref.at[mine], sems.at[slot * per + i]
            ).start()

    @pl.when(step == count - 1)
    def _():
        notes_copy().wait()
        for s in range(2):
            for i in range(per):
                pltpu.make_async_copy(
                    stage.at[s, i], second_ref.at[0], sems.at[s * per + i]
                ).wait()


def prep(where, intensity, groups):
    frames = intensity.shape[0]
    per = 4
    return pl.pallas_call(
        prep_kernel,
        grid_spec=pltpu.PrefetchScalarGridSpec(
            num_scalar_prefetch=1,
            grid=(frames // per,),
            in_specs=[
                pl.BlockSpec((per, FRAME, FRAME), lambda s, w: (s, 0, 0)),
                pl.BlockSpec((FRAME, FRAME), lambda s, w: (0, 0)),
            ],
            out_specs=[pl.BlockSpec(memory_space=pl.ANY)] * 2,
            scratch_shapes=[
                pltpu.VMEM((2, per, 2 * FRAME, 128), BF16),
                pltpu.VMEM((per, 2, FRAME, 128), F32),
                pltpu.VMEM((groups, NOTE_ROWS, 128), BF16),
                pltpu.SMEM((frames + groups,), jnp.int32),
                pltpu.SemaphoreType.DMA((2 * per + 1,)),
            ],
        ),
        out_shape=[
            jax.ShapeDtypeStruct((groups, 2 * FRAME + NOTE_ROWS, 128), BF16),
            jax.ShapeDtypeStruct((groups, 2 * FRAME, 128), BF16),
        ],
        compiler_params=pltpu.CompilerParams(vmem_limit_bytes=56 << 20),
        cost_estimate=pl.CostEstimate(
            flops=frames * 2 * FRAME**3, bytes_accessed=frames * FRAME * FRAME * 6, transcendentals=0
        ),
        name="prep",
    )(where, intensity, jnp.asarray(deinterleave()))


def tile_copies(obj_hbm, ext_ref, sems):
    return [
        pltpu.make_async_copy(
            obj_hbm.at[part, :, pl.ds(128 * j, 128)],
            ext_ref.at[part, j + 1, pl.ds(HALF, TILE), :],
            sems.at[1 + part * (TILE // 128) + j],
        )
        for part in range(2)
        for j in range(TILE // 128)
    ]


def set_halo(north_ref, south_ref, west_ref, east_ref, ext_ref):
    for part in range(2):
        ext_ref[part, 0] = west_ref[part].astype(F32)
        ext_ref[part, PANELS - 1] = east_ref[part].astype(F32)
        for j in range(TILE // 128):
            lanes = slice(128 * j, 128 * j + 128)
            ext_ref[part, j + 1, 0:HALF, :] = north_ref[part, :, lanes].astype(F32)
            ext_ref[part, j + 1, HALF + TILE :, :] = south_ref[part, :, lanes].astype(F32)


def rows_of(m, p=0, height=FRAME):
    return slice(FRAME * m + HALF * p, FRAME * m + HALF * p + height)


def forward(places, probe_ref, table_ref, ext_ref, xs, gs, take):
    members = range(len(places))
    lane = lax.broadcasted_iota(jnp.int32, (FRAME, 128), 1)
    for m in members:
        row, col, live = places[m]
        panel = col // 128
        shift = col % 128
        back_shift = (128 - shift) % 128
        keep = lane < 128 - shift

        def cut(part):
            rolled = [
                pltpu.roll(ext_ref[part, panel + i, pl.ds(row, FRAME), :], back_shift, 1)
                for i in range(3)
            ]
            return [jnp.where(keep, rolled[i], rolled[i + 1]) for i in range(2)]

        patch_re = cut(0)
        patch_im = cut(1)
        ex_re, ex_im = [], []
        for h in range(2):
            lanes = slice(128 * h, 128 * h + 128)
            pr = probe_ref[0, :, lanes]
            pi = probe_ref[1, :, lanes]
            ex_re.append(pr * patch_re[h] - pi * patch_im[h])
            ex_im.append(pr * patch_im[h] + pi * patch_re[h])
        xs[0, rows_of(m), 0:128] = (ex_re[0] + ex_re[1]).astype(BF16)
        xs[0, rows_of(m), 128:256] = (ex_im[0] + ex_im[1]).astype(BF16)
        xs[1, rows_of(m), 0:128] = (ex_re[0] - ex_re[1]).astype(BF16)
        xs[1, rows_of(m), 128:256] = (ex_im[0] - ex_im[1]).astype(BF16)
    halves = [dot(xs[q], table_ref[q]) for q in range(2)]
    for m in members:
        for q in range(2):
            half = halves[q][rows_of(m)]
            top, bottom = half[:HALF], half[HALF:]
            lanes = slice(128 * q, 128 * q + 128)
            for p, fold in ((0, top + bottom), (1, top - bottom)):
                folded = fold.astype(BF16)
                gs[m, p, 0:HALF, lanes] = folded[:, :128]
                gs[m, p, HALF:, lanes] = folded[:, 128:]
    for m in members:
        for p in range(2):
            take(m, p, dot(table_ref[2 + p], gs[m, p]))


def update(m, p, far, amp_ref, ds):
    for q in range(2):
        lanes = slice(128 * q, 128 * q + 128)
        far_re, far_im = far[:HALF, lanes], far[HALF:, lanes]
        a = amp_ref[m, FRAME * q + HALF * p : FRAME * q + HALF * p + HALF, :].astype(F32)
        factor = a * lax.rsqrt(far_re * far_re + far_im * far_im + 1.0) - 1.0
        ds[q, rows_of(m, p, HALF), 0:128] = (far_re * factor).astype(BF16)
        ds[q, rows_of(m, p, HALF), 128:256] = (far_im * factor).astype(BF16)


def backward(places, probe_ref, table_ref, acc_ref, ds, ms):
    members = range(len(places))
    lane = lax.broadcasted_iota(jnp.int32, (HALF, 128), 1)
    evens = dot(ds[0], table_ref[4])
    odds = dot(ds[1], table_ref[5])
    for m in members:
        even, odd = evens[rows_of(m)], odds[rows_of(m)]
        for h, mid in ((0, (even + odd).astype(BF16)), (1, (even - odd).astype(BF16))):
            lanes = slice(128 * h, 128 * h + 128)
            for p in range(2):
                rows = slice(HALF * p, HALF * p + HALF)
                ms[m, p, 0:HALF, lanes] = mid[rows, :128]
                ms[m, p, HALF:, lanes] = mid[rows, 128:]
    for m in members:
        row, col, live = places[m]
        shift = col % 128
        panel = jnp.where(live > 0, col // 128, PANELS)
        even = dot(table_ref[6], ms[m, 0])
        odd = dot(table_ref[7], ms[m, 1])
        keep = lane < shift
        for v in range(2):
            back = even + odd if v == 0 else even - odd
            back_re, back_im = back[:HALF], back[HALF:]
            rows = slice(HALF * v, HALF * v + HALF)
            pr = probe_ref[0, rows]
            pi = probe_ref[1, rows]
            where = pl.ds(row + HALF * v, HALF)
            for part, term in ((0, pr * back_re + pi * back_im), (1, pr * back_im - pi * back_re)):
                left = pltpu.roll(term[:, :128], shift, 1)
                right = pltpu.roll(term[:, 128:], shift, 1)
                acc_ref[part, panel, where, :] += jnp.where(keep, 0.0, left)
                acc_ref[part, panel + 1, where, :] += jnp.where(keep, left, right)
                acc_ref[part, panel + 2, where, :] += jnp.where(keep, right, 0.0)


def places_of(meta_ref, rank, group):
    places = [[meta_ref[3 * rank + k, group * GROUP + m] for k in range(3)] for m in range(GROUP)]
    live = places[0][2]
    for place in places[1:]:
        live = live + place[2]
    return places, live > 0


def first_kernel(
    meta_ref, amp_ref, probe_ref, table_ref, north_ref, south_ref, west_ref, east_ref, obj_hbm,
    out_hbm, far_ref, ext_ref, acc_ref, sems, xs, gs, ds, ms,
):
    step = pl.program_id(0)
    groups = pl.num_programs(0) // 2

    def save():
        return pltpu.make_async_copy(acc_ref.at[:, pl.ds(0, PANELS)], out_hbm, sems.at[0])

    @pl.when(step == 0)
    def _():
        copies = tile_copies(obj_hbm, ext_ref, sems)
        for copy in copies:
            copy.start()
        acc_ref[:, 0:PANELS] = jnp.zeros_like(ext_ref)
        set_halo(north_ref, south_ref, west_ref, east_ref, ext_ref)
        for copy in copies:
            copy.wait()
        inner = slice(HALF, HALF + TILE)
        acc_ref[:, 1 : PANELS - 1, inner, :] = 2.0 * ext_ref[:, 1 : PANELS - 1, inner, :]

    places, live = places_of(meta_ref, 0, jnp.minimum(step, groups - 1))

    @pl.when(live & (step < groups))
    def _():
        def take(m, p, far):
            update(m, p, far, amp_ref, ds)

        forward(places, probe_ref, table_ref, ext_ref, xs, gs, take)
        backward(places, probe_ref, table_ref, acc_ref, ds, ms)

    @pl.when(step == groups - 1)
    def _():
        save().start()

    later, live = places_of(meta_ref, 1, jnp.maximum(step - groups, 0))

    @pl.when(live & (step >= groups))
    def _():
        def take(m, p, far):
            far_ref[m, p] = far.astype(BF16)

        forward(later, probe_ref, table_ref, ext_ref, xs, gs, take)

    @pl.when(step == pl.num_programs(0) - 1)
    def _():
        save().wait()


def last_kernel(
    meta_ref, amp_ref, far_ref, probe_ref, table_ref, start_hbm,
    west_ref, east_ref, top_ref, bottom_ref, inner_ref, acc_ref, start_ref, sems, ds, ms,
):
    step = pl.program_id(0)

    def load():
        return pltpu.make_async_copy(start_hbm, start_ref, sems.at[0])

    @pl.when(step == 0)
    def _():
        load().start()
        acc_ref[:, 0:PANELS] = jnp.zeros_like(start_ref)

    places, live = places_of(meta_ref, 1, step)

    @pl.when(live)
    def _():
        for m in range(GROUP):
            for p in range(2):
                update(m, p, far_ref[m, p].astype(F32), amp_ref, ds)
        backward(places, probe_ref, table_ref, acc_ref, ds, ms)

    @pl.when(step == pl.num_programs(0) - 1)
    def _():
        load().wait()

        def half_sum(part, panel, rows):
            return 0.5 * (acc_ref[part, panel, rows, :] + start_ref[part, panel, rows, :])

        for part in range(2):
            west_ref[part] = half_sum(part, 0, slice(0, EXTENT)).astype(BF16)
            east_ref[part] = half_sum(part, PANELS - 1, slice(0, EXTENT)).astype(BF16)
            for j in range(TILE // 128):
                lanes = slice(128 * j, 128 * j + 128)
                top_ref[part, :, lanes] = half_sum(part, j + 1, slice(0, HALF)).astype(BF16)
                inner_ref[part, :, lanes] = half_sum(part, j + 1, slice(HALF, HALF + TILE))
                rows = slice(HALF + TILE, EXTENT)
                bottom_ref[part, :, lanes] = half_sum(part, j + 1, rows).astype(BF16)


def whole(shape):
    return pl.BlockSpec(shape, lambda s, m: (0,) * len(shape))


WIDE = (2, PANELS, EXTENT, 128)
SUMS = (2, PANELS + 3, EXTENT, 128)
FLAT = (2, GROUP * FRAME, FRAME)
DEEP = (GROUP, 2, FRAME, FRAME)


def run_first(meta, amps, probe, tabs, obj, north, south, west, east):
    groups = amps.shape[0] // GROUP
    return pl.pallas_call(
        first_kernel,
        grid_spec=pltpu.PrefetchScalarGridSpec(
            num_scalar_prefetch=1,
            grid=(2 * groups,),
            in_specs=[
                pl.BlockSpec(
                    (GROUP,) + amps.shape[1:], lambda s, m: (jnp.minimum(s, groups - 1), 0, 0)
                ),
                whole((2, FRAME, FRAME)),
                whole((8, FRAME, FRAME)),
                whole(north.shape),
                whole(south.shape),
                whole(west.shape),
                whole(east.shape),
                pl.BlockSpec(memory_space=pl.ANY),
            ],
            out_specs=[
                pl.BlockSpec(memory_space=pl.ANY),
                pl.BlockSpec(DEEP, lambda s, m: (jnp.maximum(s - groups, 0), 0, 0, 0)),
            ],
            scratch_shapes=[
                pltpu.VMEM(WIDE, F32),
                pltpu.VMEM(SUMS, F32),
                pltpu.SemaphoreType.DMA((1 + 2 * TILE // 128,)),
            ]
            + [pltpu.VMEM(shape, BF16) for shape in (FLAT, DEEP, FLAT, DEEP)],
        ),
        out_shape=[
            jax.ShapeDtypeStruct(WIDE, F32),
            jax.ShapeDtypeStruct((amps.shape[0], 2, FRAME, FRAME), BF16),
        ],
        compiler_params=pltpu.CompilerParams(vmem_limit_bytes=50 << 20),
        cost_estimate=pl.CostEstimate(
            flops=2 * amps.shape[0] * 16 * FRAME**3, bytes_accessed=24 << 20, transcendentals=0
        ),
        name="first",
    )(meta, amps, probe, tabs, north, south, west, east, obj)


def run_last(meta, amps, far, probe, tabs, start):
    groups = amps.shape[0] // GROUP

    def used(s, m):
        live = m[5, s * GROUP]
        for k in range(1, GROUP):
            live = live + m[5, s * GROUP + k]
        return jnp.where(live > 0, s, 0)

    shapes = [(2, EXTENT, 128)] * 2 + [(2, HALF, TILE)] * 2 + [(2, TILE, TILE)]
    return pl.pallas_call(
        last_kernel,
        grid_spec=pltpu.PrefetchScalarGridSpec(
            num_scalar_prefetch=1,
            grid=(groups,),
            in_specs=[
                pl.BlockSpec((GROUP,) + amps.shape[1:], lambda s, m: (used(s, m), 0, 0)),
                pl.BlockSpec(DEEP, lambda s, m: (used(s, m), 0, 0, 0)),
                whole((2, FRAME, FRAME)),
                whole((8, FRAME, FRAME)),
                pl.BlockSpec(memory_space=pl.ANY),
            ],
            out_specs=[whole(shape) for shape in shapes],
            scratch_shapes=[
                pltpu.VMEM(SUMS, F32),
                pltpu.VMEM(WIDE, F32),
                pltpu.SemaphoreType.DMA((1,)),
                pltpu.VMEM(FLAT, BF16),
                pltpu.VMEM(DEEP, BF16),
            ],
        ),
        out_shape=[jax.ShapeDtypeStruct(s, d) for s, d in zip(shapes, (BF16,) * 4 + (F32,))],
        compiler_params=pltpu.CompilerParams(vmem_limit_bytes=54 << 20),
        cost_estimate=pl.CostEstimate(
            flops=amps.shape[0] * 8 * FRAME**3, bytes_accessed=20 << 20, transcendentals=0
        ),
        name="last",
    )(meta, amps, far, probe, tabs, start)


def across_kernel(top_ref, bottom_ref, west_n, west_s, east_n, east_s, north_ref, south_ref):
    for base, west, east, out in (
        (top_ref, west_n, east_n, north_ref), (bottom_ref, west_s, east_s, south_ref)
    ):
        out[:, :, 0:HALF] = (base[:, :, 0:HALF].astype(F32) + west[...].astype(F32)).astype(BF16)
        out[:, :, HALF : TILE - HALF] = base[:, :, HALF : TILE - HALF]
        out[:, :, TILE - HALF :] = (base[:, :, TILE - HALF :].astype(F32) + east[...].astype(F32)).astype(BF16)


def across(top, bottom, from_west, from_east):
    end = EXTENT // HALF - 1
    full = pl.BlockSpec((2, HALF, TILE), lambda i: (0, 0, 0))
    first = pl.BlockSpec((2, HALF, 128), lambda i: (0, 0, 0))
    last = pl.BlockSpec((2, HALF, 128), lambda i: (0, end, 0))
    return pl.pallas_call(
        across_kernel,
        grid=(1,),
        in_specs=[full, full, first, last, first, last],
        out_specs=[full, full],
        out_shape=[jax.ShapeDtypeStruct((2, HALF, TILE), BF16)] * 2,
        compiler_params=pltpu.CompilerParams(vmem_limit_bytes=50 << 20),
        name="across",
    )(top, bottom, from_west, from_west, from_east, from_east)


def sides_kernel(base_ref, west_ref, east_ref, out_ref):
    inner = slice(HALF, HALF + TILE)

    @pl.when(pl.program_id(0) == 0)
    def _():
        out_ref[...] = base_ref[...] + west_ref[:, inner, :].astype(F32)

    @pl.when(pl.program_id(0) == 1)
    def _():
        out_ref[...] = base_ref[...] + east_ref[:, inner, :].astype(F32)


def ends_kernel(base_ref, north_ref, south_ref, out_ref):
    @pl.when(pl.program_id(0) == 0)
    def _():
        out_ref[...] = base_ref[...] + north_ref[...].astype(F32)

    @pl.when(pl.program_id(0) == 1)
    def _():
        out_ref[...] = base_ref[...] + south_ref[...].astype(F32)


def add_pair(kernel, base, block, place, low, high):
    strip = pl.BlockSpec(low.shape, lambda i: (0, 0, 0))
    return pl.pallas_call(
        kernel,
        grid=(2,),
        in_specs=[pl.BlockSpec(block, place), strip, strip],
        out_specs=pl.BlockSpec(block, place),
        out_shape=jax.ShapeDtypeStruct(base.shape, F32),
        input_output_aliases={0: 0},
        compiler_params=pltpu.CompilerParams(vmem_limit_bytes=50 << 20),
        name="ends",
    )(base, low, high)


def shifted(value, axis, by):
    size = lax.axis_size(axis)
    pairs = [(i, i + by) for i in range(size) if 0 <= i + by < size]
    return lax.ppermute(value, axis, pairs)


def body(obj, probe, intensity, dest, offsets):
    groups = lax.axis_size("gx")
    sends = prep(jnp.concatenate([dest.T, offsets.T]).reshape(-1), intensity, groups)
    north = shifted(obj[:, TILE - HALF :, :].astype(BF16), "gy", 1)
    south = shifted(obj[:, :HALF, :].astype(BF16), "gy", -1)
    routed = functools.partial(
        lax.all_to_all, axis_name="gx", split_axis=0, concat_axis=0, tiled=True
    )
    first, north, south = lax.optimization_barrier((sends[0], north, south))
    amps = routed(first)

    def column(lo, hi):
        own = obj[:, :, lo:hi].astype(BF16)
        return jnp.concatenate([north[:, :, lo:hi], own, south[:, :, lo:hi]], axis=1)

    west = shifted(column(TILE - HALF, TILE), "gx", 1)
    east = shifted(column(0, HALF), "gx", -1)
    west, east, rest = lax.optimization_barrier((west, east, sends[1]))
    more = routed(rest)
    tabs = jnp.asarray(table_blocks())
    notes = amps[:, 2 * FRAME, :10].astype(jnp.int32).T
    meta = jnp.stack(
        [
            notes[5 * r] * 16 + notes[5 * r + 1] if k == 0 else
            notes[5 * r + 2] * 16 + notes[5 * r + 3] if k == 1 else notes[5 * r + 4]
            for r in range(CAP) for k in range(3)
        ]
    )
    acc, far = run_first(meta, amps, probe, tabs, obj, north, south, west, east)
    west, east, top, bottom, inner = run_last(meta, more, far, probe, tabs, acc)
    from_west = shifted(east, "gx", 1)
    from_east = shifted(west, "gx", -1)
    to_north, to_south = across(top, bottom, from_west, from_east)
    from_north = shifted(to_south, "gy", 1)
    from_south = shifted(to_north, "gy", -1)
    steps = TILE // HALF - 1
    inner = add_pair(
        sides_kernel, inner, (2, TILE, HALF), lambda i: (0, 0, steps * i), from_west, from_east
    )
    return add_pair(
        ends_kernel, inner, (2, HALF, TILE), lambda i: (0, steps * i, 0), from_north, from_south
    )


def solution(mesh):
    placed = (
        P(None, "gy", "gx"),
        P(),
        P(("gx", "gy"), None, None),
        P(("gx", "gy"), None),
        P(("gx", "gy"), None),
    )
    return jax.shard_map(
        body, mesh=mesh, in_specs=placed, out_specs=P(None, "gy", "gx"), check_vma=False
    )
```

```python
import functools
import math

import jax
import jax.numpy as jnp
import numpy as np
from jax import lax
from jax.experimental import pallas as pl
from jax.experimental.pallas import tpu as pltpu
from jax.sharding import PartitionSpec as P

CAP = 2
FRAME = 256
HALF = 128
TILE = 512
EXTENT = TILE + 2 * HALF
PANELS = EXTENT // 128
NOTE_ROWS = 16
GROUP = 4
BF16 = jnp.bfloat16
F32 = jnp.float32


def table_blocks():
    index = np.arange(FRAME)[:, None] * np.arange(FRAME)[None, :] % FRAME
    angle = index.astype(np.float32) * np.float32(2.0 * math.pi / FRAME)
    scale = np.float32(1.0 / math.sqrt(FRAME))
    re = (np.cos(angle) * scale).astype(BF16)
    im = (-np.sin(angle) * scale).astype(BF16)
    blocks = []
    for parity in (0, 1):
        c = re[:HALF, parity::2]
        s = im[:HALF, parity::2]
        fwd_right = np.block([[c, s], [-s, c]])
        fwd_left = fwd_right.T
        inv_right = np.block([[c.T, -s.T], [s.T, c.T]])
        inv_left = inv_right.T
        blocks.append([fwd_right, fwd_left, inv_right, inv_left])
    return np.stack([blocks[p][i] for i in range(4) for p in (0, 1)]).astype(BF16)


def deinterleave():
    perm = np.zeros((FRAME, FRAME), np.float32)
    for j in range(HALF):
        perm[2 * j, j] = 1.0
        perm[2 * j + 1, HALF + j] = 1.0
    return perm.astype(BF16)


def dot(a, b):
    return jnp.dot(a, b, preferred_element_type=F32)


def prep_kernel(
    where_ref, inten_ref, perm_ref, first_ref, second_ref, stage, split, notes, ranks, sems
):
    step = pl.program_id(0)
    count = pl.num_programs(0)
    per = inten_ref.shape[0]
    groups = first_ref.shape[0]
    slot = step % 2

    def notes_copy():
        return pltpu.make_async_copy(
            notes, first_ref.at[:, pl.ds(2 * FRAME, NOTE_ROWS), :], sems.at[2 * per]
        )

    @pl.when(step == 0)
    def _():
        lane = lax.broadcasted_iota(jnp.int32, (groups, 128), 1)
        owner = lax.broadcasted_iota(jnp.int32, (groups, 128), 0)
        note = jnp.zeros((groups, 128), jnp.int32)
        for g in range(groups):
            ranks[per * count + g] = 0
        for f in range(per * count):
            mine = where_ref[f]
            rank = ranks[per * count + mine]
            ranks[f] = rank
            ranks[per * count + mine] = rank + 1
            row, col = where_ref[per * count + f], where_ref[2 * per * count + f]
            at = lane - 5 * rank
            value = jnp.where(at == 0, row // 16, jnp.where(at == 1, row % 16, 0))
            value += jnp.where(at == 2, col // 16, jnp.where(at == 3, col % 16, 0))
            value += jnp.where(at == 4, 1, 0)
            note = jnp.where(owner == mine, note + value, note)
        notes[...] = jnp.broadcast_to(note.astype(F32)[:, None, :], notes.shape).astype(BF16)
        notes_copy().start()

    for i in range(per):

        @pl.when(step >= 2)
        def _():
            pltpu.make_async_copy(
                stage.at[slot, i], second_ref.at[0], sems.at[slot * per + i]
            ).wait()

    for i in range(per):
        for h in range(2):
            split[i, h] = jnp.sqrt(inten_ref[i, :, 128 * h : 128 * h + 128])
        rows = [
            jnp.concatenate([split[i, h, pl.ds(p, HALF, 2), :] for h in range(2)], axis=1)
            for p in range(2)
        ]
        amp = jnp.concatenate(rows, axis=0).astype(BF16)
        cols = dot(amp, perm_ref[...]).astype(BF16)
        stage[slot, i, 0:FRAME, :] = cols[:, :128]
        stage[slot, i, FRAME : 2 * FRAME, :] = cols[:, 128:]
    for i in range(per):
        f = step * per + i
        mine = where_ref[f]
        rank = ranks[f]

        @pl.when(rank == 0)
        def _():
            pltpu.make_async_copy(
                stage.at[slot, i],
                first_ref.at[mine, pl.ds(0, 2 * FRAME), :],
                sems.at[slot * per + i],
            ).start()

        @pl.when(rank != 0)
        def _():
            pltpu.make_async_copy(
                stage.at[slot, i], second_ref.at[mine], sems.at[slot * per + i]
            ).start()

    @pl.when(step == count - 1)
    def _():
        notes_copy().wait()
        for s in range(2):
            for i in range(per):
                pltpu.make_async_copy(
                    stage.at[s, i], second_ref.at[0], sems.at[s * per + i]
                ).wait()


def prep(where, intensity, groups):
    frames = intensity.shape[0]
    per = 8
    return pl.pallas_call(
        prep_kernel,
        grid_spec=pltpu.PrefetchScalarGridSpec(
            num_scalar_prefetch=1,
            grid=(frames // per,),
            in_specs=[
                pl.BlockSpec((per, FRAME, FRAME), lambda s, w: (s, 0, 0)),
                pl.BlockSpec((FRAME, FRAME), lambda s, w: (0, 0)),
            ],
            out_specs=[pl.BlockSpec(memory_space=pl.ANY)] * 2,
            scratch_shapes=[
                pltpu.VMEM((2, per, 2 * FRAME, 128), BF16),
                pltpu.VMEM((per, 2, FRAME, 128), F32),
                pltpu.VMEM((groups, NOTE_ROWS, 128), BF16),
                pltpu.SMEM((frames + groups,), jnp.int32),
                pltpu.SemaphoreType.DMA((2 * per + 1,)),
            ],
        ),
        out_shape=[
            jax.ShapeDtypeStruct((groups, 2 * FRAME + NOTE_ROWS, 128), BF16),
            jax.ShapeDtypeStruct((groups, 2 * FRAME, 128), BF16),
        ],
        compiler_params=pltpu.CompilerParams(vmem_limit_bytes=56 << 20),
        cost_estimate=pl.CostEstimate(
            flops=frames * 2 * FRAME**3, bytes_accessed=frames * FRAME * FRAME * 6, transcendentals=0
        ),
        name="prep",
    )(where, intensity, jnp.asarray(deinterleave()))


def tile_copies(obj_hbm, ext_ref, sems):
    return [
        pltpu.make_async_copy(
            obj_hbm.at[part, :, pl.ds(128 * j, 128)],
            ext_ref.at[part, j + 1, pl.ds(HALF, TILE), :],
            sems.at[1 + part * (TILE // 128) + j],
        )
        for part in range(2)
        for j in range(TILE // 128)
    ]


def set_halo(north_ref, south_ref, west_ref, east_ref, ext_ref):
    for part in range(2):
        ext_ref[part, 0] = west_ref[part].astype(F32)
        ext_ref[part, PANELS - 1] = east_ref[part].astype(F32)
        for j in range(TILE // 128):
            lanes = slice(128 * j, 128 * j + 128)
            ext_ref[part, j + 1, 0:HALF, :] = north_ref[part, :, lanes].astype(F32)
            ext_ref[part, j + 1, HALF + TILE :, :] = south_ref[part, :, lanes].astype(F32)


def rows_of(m, p=0, height=FRAME):
    return slice(FRAME * m + HALF * p, FRAME * m + HALF * p + height)


def forward(places, probe_ref, table_ref, ext_ref, xs, gs, take):
    members = range(len(places))
    lane = lax.broadcasted_iota(jnp.int32, (FRAME, 128), 1)
    for m in members:
        row, col, live = places[m]
        panel = col // 128
        shift = col % 128
        back_shift = (128 - shift) % 128
        keep = lane < 128 - shift

        def cut(part):
            rolled = [
                pltpu.roll(ext_ref[part, panel + i, pl.ds(row, FRAME), :], back_shift, 1)
                for i in range(3)
            ]
            return [jnp.where(keep, rolled[i], rolled[i + 1]) for i in range(2)]

        patch_re = cut(0)
        patch_im = cut(1)
        ex_re, ex_im = [], []
        for h in range(2):
            lanes = slice(128 * h, 128 * h + 128)
            pr = probe_ref[0, :, lanes]
            pi = probe_ref[1, :, lanes]
            ex_re.append(pr * patch_re[h] - pi * patch_im[h])
            ex_im.append(pr * patch_im[h] + pi * patch_re[h])
        xs[0, rows_of(m), 0:128] = (ex_re[0] + ex_re[1]).astype(BF16)
        xs[0, rows_of(m), 128:256] = (ex_im[0] + ex_im[1]).astype(BF16)
        xs[1, rows_of(m), 0:128] = (ex_re[0] - ex_re[1]).astype(BF16)
        xs[1, rows_of(m), 128:256] = (ex_im[0] - ex_im[1]).astype(BF16)
    halves = [dot(xs[q], table_ref[q]) for q in range(2)]
    for m in members:
        for q in range(2):
            half = halves[q][rows_of(m)]
            top, bottom = half[:HALF], half[HALF:]
            lanes = slice(128 * q, 128 * q + 128)
            for p, fold in ((0, top + bottom), (1, top - bottom)):
                folded = fold.astype(BF16)
                gs[m, p, 0:HALF, lanes] = folded[:, :128]
                gs[m, p, HALF:, lanes] = folded[:, 128:]
    for m in members:
        for p in range(2):
            take(m, p, dot(table_ref[2 + p], gs[m, p]))


def update(m, p, far, amp_ref, ds):
    for q in range(2):
        lanes = slice(128 * q, 128 * q + 128)
        far_re, far_im = far[:HALF, lanes], far[HALF:, lanes]
        a = amp_ref[m, FRAME * q + HALF * p : FRAME * q + HALF * p + HALF, :].astype(F32)
        factor = a * lax.rsqrt(far_re * far_re + far_im * far_im + 1.0) - 1.0
        ds[q, rows_of(m, p, HALF), 0:128] = (far_re * factor).astype(BF16)
        ds[q, rows_of(m, p, HALF), 128:256] = (far_im * factor).astype(BF16)


def backward(places, probe_ref, table_ref, acc_ref, ds, ms):
    members = range(len(places))
    lane = lax.broadcasted_iota(jnp.int32, (HALF, 128), 1)
    evens = dot(ds[0], table_ref[4])
    odds = dot(ds[1], table_ref[5])
    for m in members:
        even, odd = evens[rows_of(m)], odds[rows_of(m)]
        for h, mid in ((0, (even + odd).astype(BF16)), (1, (even - odd).astype(BF16))):
            lanes = slice(128 * h, 128 * h + 128)
            for p in range(2):
                rows = slice(HALF * p, HALF * p + HALF)
                ms[m, p, 0:HALF, lanes] = mid[rows, :128]
                ms[m, p, HALF:, lanes] = mid[rows, 128:]
    for m in members:
        row, col, live = places[m]
        shift = col % 128
        panel = jnp.where(live > 0, col // 128, PANELS)
        even = dot(table_ref[6], ms[m, 0])
        odd = dot(table_ref[7], ms[m, 1])
        keep = lane < shift
        for v in range(2):
            back = even + odd if v == 0 else even - odd
            back_re, back_im = back[:HALF], back[HALF:]
            rows = slice(HALF * v, HALF * v + HALF)
            pr = probe_ref[0, rows]
            pi = probe_ref[1, rows]
            where = pl.ds(row + HALF * v, HALF)
            for part, term in ((0, pr * back_re + pi * back_im), (1, pr * back_im - pi * back_re)):
                left = pltpu.roll(term[:, :128], shift, 1)
                right = pltpu.roll(term[:, 128:], shift, 1)
                acc_ref[part, panel, where, :] += jnp.where(keep, 0.0, left)
                acc_ref[part, panel + 1, where, :] += jnp.where(keep, left, right)
                acc_ref[part, panel + 2, where, :] += jnp.where(keep, right, 0.0)


def places_of(meta_ref, rank, group):
    places = [[meta_ref[3 * rank + k, group * GROUP + m] for k in range(3)] for m in range(GROUP)]
    live = places[0][2]
    for place in places[1:]:
        live = live + place[2]
    return places, live > 0


def first_kernel(
    meta_ref, amp_ref, probe_ref, table_ref, north_ref, south_ref, west_ref, east_ref, obj_hbm,
    out_hbm, far_ref, ext_ref, acc_ref, sems, xs, gs, ds, ms,
):
    step = pl.program_id(0)
    groups = pl.num_programs(0) // 2

    def save():
        return pltpu.make_async_copy(acc_ref.at[:, pl.ds(0, PANELS)], out_hbm, sems.at[0])

    @pl.when(step == 0)
    def _():
        copies = tile_copies(obj_hbm, ext_ref, sems)
        for copy in copies:
            copy.start()
        acc_ref[:, 0:PANELS] = jnp.zeros_like(ext_ref)
        set_halo(north_ref, south_ref, west_ref, east_ref, ext_ref)
        for copy in copies:
            copy.wait()
        inner = slice(HALF, HALF + TILE)
        acc_ref[:, 1 : PANELS - 1, inner, :] = 2.0 * ext_ref[:, 1 : PANELS - 1, inner, :]

    places, live = places_of(meta_ref, 0, jnp.minimum(step, groups - 1))

    @pl.when(live & (step < groups))
    def _():
        def take(m, p, far):
            update(m, p, far, amp_ref, ds)

        forward(places, probe_ref, table_ref, ext_ref, xs, gs, take)
        backward(places, probe_ref, table_ref, acc_ref, ds, ms)

    @pl.when(step == groups - 1)
    def _():
        save().start()

    later, live = places_of(meta_ref, 1, jnp.maximum(step - groups, 0))

    @pl.when(live & (step >= groups))
    def _():
        def take(m, p, far):
            far_ref[m, p] = far.astype(BF16)

        forward(later, probe_ref, table_ref, ext_ref, xs, gs, take)

    @pl.when(step == pl.num_programs(0) - 1)
    def _():
        save().wait()


def last_kernel(
    meta_ref, amp_ref, far_ref, probe_ref, table_ref, start_hbm,
    west_ref, east_ref, top_ref, bottom_ref, inner_ref, acc_ref, start_ref, sems, ds, ms,
):
    step = pl.program_id(0)

    def load():
        return pltpu.make_async_copy(start_hbm, start_ref, sems.at[0])

    @pl.when(step == 0)
    def _():
        load().start()
        acc_ref[:, 0:PANELS] = jnp.zeros_like(start_ref)

    places, live = places_of(meta_ref, 1, step)

    @pl.when(live)
    def _():
        for m in range(GROUP):
            for p in range(2):
                update(m, p, far_ref[m, p].astype(F32), amp_ref, ds)
        backward(places, probe_ref, table_ref, acc_ref, ds, ms)

    @pl.when(step == pl.num_programs(0) - 1)
    def _():
        load().wait()

        def half_sum(part, panel, rows):
            return 0.5 * (acc_ref[part, panel, rows, :] + start_ref[part, panel, rows, :])

        for part in range(2):
            west_ref[part] = half_sum(part, 0, slice(0, EXTENT)).astype(BF16)
            east_ref[part] = half_sum(part, PANELS - 1, slice(0, EXTENT)).astype(BF16)
            for j in range(TILE // 128):
                lanes = slice(128 * j, 128 * j + 128)
                top_ref[part, :, lanes] = half_sum(part, j + 1, slice(0, HALF)).astype(BF16)
                inner_ref[part, :, lanes] = half_sum(part, j + 1, slice(HALF, HALF + TILE))
                rows = slice(HALF + TILE, EXTENT)
                bottom_ref[part, :, lanes] = half_sum(part, j + 1, rows).astype(BF16)


def whole(shape):
    return pl.BlockSpec(shape, lambda s, m: (0,) * len(shape))


WIDE = (2, PANELS, EXTENT, 128)
SUMS = (2, PANELS + 3, EXTENT, 128)
FLAT = (2, GROUP * FRAME, FRAME)
DEEP = (GROUP, 2, FRAME, FRAME)


def run_first(meta, amps, probe, tabs, obj, north, south, west, east):
    groups = amps.shape[0] // GROUP
    return pl.pallas_call(
        first_kernel,
        grid_spec=pltpu.PrefetchScalarGridSpec(
            num_scalar_prefetch=1,
            grid=(2 * groups,),
            in_specs=[
                pl.BlockSpec(
                    (GROUP,) + amps.shape[1:], lambda s, m: (jnp.minimum(s, groups - 1), 0, 0)
                ),
                whole((2, FRAME, FRAME)),
                whole((8, FRAME, FRAME)),
                whole(north.shape),
                whole(south.shape),
                whole(west.shape),
                whole(east.shape),
                pl.BlockSpec(memory_space=pl.ANY),
            ],
            out_specs=[
                pl.BlockSpec(memory_space=pl.ANY),
                pl.BlockSpec(DEEP, lambda s, m: (jnp.maximum(s - groups, 0), 0, 0, 0)),
            ],
            scratch_shapes=[
                pltpu.VMEM(WIDE, F32),
                pltpu.VMEM(SUMS, F32),
                pltpu.SemaphoreType.DMA((1 + 2 * TILE // 128,)),
            ]
            + [pltpu.VMEM(shape, BF16) for shape in (FLAT, DEEP, FLAT, DEEP)],
        ),
        out_shape=[
            jax.ShapeDtypeStruct(WIDE, F32),
            jax.ShapeDtypeStruct((amps.shape[0], 2, FRAME, FRAME), BF16),
        ],
        compiler_params=pltpu.CompilerParams(vmem_limit_bytes=50 << 20),
        cost_estimate=pl.CostEstimate(
            flops=2 * amps.shape[0] * 16 * FRAME**3, bytes_accessed=24 << 20, transcendentals=0
        ),
        name="first",
    )(meta, amps, probe, tabs, north, south, west, east, obj)


def run_last(meta, amps, far, probe, tabs, start):
    groups = amps.shape[0] // GROUP

    def used(s, m):
        live = m[5, s * GROUP]
        for k in range(1, GROUP):
            live = live + m[5, s * GROUP + k]
        return jnp.where(live > 0, s, 0)

    shapes = [(2, EXTENT, 128)] * 2 + [(2, HALF, TILE)] * 2 + [(2, TILE, TILE)]
    return pl.pallas_call(
        last_kernel,
        grid_spec=pltpu.PrefetchScalarGridSpec(
            num_scalar_prefetch=1,
            grid=(groups,),
            in_specs=[
                pl.BlockSpec((GROUP,) + amps.shape[1:], lambda s, m: (used(s, m), 0, 0)),
                pl.BlockSpec(DEEP, lambda s, m: (used(s, m), 0, 0, 0)),
                whole((2, FRAME, FRAME)),
                whole((8, FRAME, FRAME)),
                pl.BlockSpec(memory_space=pl.ANY),
            ],
            out_specs=[whole(shape) for shape in shapes],
            scratch_shapes=[
                pltpu.VMEM(SUMS, F32),
                pltpu.VMEM(WIDE, F32),
                pltpu.SemaphoreType.DMA((1,)),
                pltpu.VMEM(FLAT, BF16),
                pltpu.VMEM(DEEP, BF16),
            ],
        ),
        out_shape=[jax.ShapeDtypeStruct(s, d) for s, d in zip(shapes, (BF16,) * 4 + (F32,))],
        compiler_params=pltpu.CompilerParams(vmem_limit_bytes=54 << 20),
        cost_estimate=pl.CostEstimate(
            flops=amps.shape[0] * 8 * FRAME**3, bytes_accessed=20 << 20, transcendentals=0
        ),
        name="last",
    )(meta, amps, far, probe, tabs, start)


def across(base, from_west, from_east):
    left = base[:, :, :HALF].astype(F32) + from_west.astype(F32)
    right = base[:, :, TILE - HALF :].astype(F32) + from_east.astype(F32)
    return jnp.concatenate(
        [left.astype(BF16), base[:, :, HALF : TILE - HALF], right.astype(BF16)], axis=2
    )


def sides_kernel(base_ref, west_ref, east_ref, out_ref):
    inner = slice(HALF, HALF + TILE)

    @pl.when(pl.program_id(0) == 0)
    def _():
        out_ref[...] = base_ref[...] + west_ref[:, inner, :].astype(F32)

    @pl.when(pl.program_id(0) == 1)
    def _():
        out_ref[...] = base_ref[...] + east_ref[:, inner, :].astype(F32)


def ends_kernel(base_ref, north_ref, south_ref, out_ref):
    @pl.when(pl.program_id(0) == 0)
    def _():
        out_ref[...] = base_ref[...] + north_ref[...].astype(F32)

    @pl.when(pl.program_id(0) == 1)
    def _():
        out_ref[...] = base_ref[...] + south_ref[...].astype(F32)


def add_pair(kernel, base, block, place, low, high):
    strip = pl.BlockSpec(low.shape, lambda i: (0, 0, 0))
    return pl.pallas_call(
        kernel,
        grid=(2,),
        in_specs=[pl.BlockSpec(block, place), strip, strip],
        out_specs=pl.BlockSpec(block, place),
        out_shape=jax.ShapeDtypeStruct(base.shape, F32),
        input_output_aliases={0: 0},
        compiler_params=pltpu.CompilerParams(vmem_limit_bytes=50 << 20),
        name="ends",
    )(base, low, high)


def shifted(value, axis, by):
    size = lax.axis_size(axis)
    pairs = [(i, i + by) for i in range(size) if 0 <= i + by < size]
    return lax.ppermute(value, axis, pairs)


def body(obj, probe, intensity, dest, offsets):
    groups = lax.axis_size("gx")
    sends = prep(jnp.concatenate([dest.T, offsets.T]).reshape(-1), intensity, groups)
    north = shifted(obj[:, TILE - HALF :, :].astype(BF16), "gy", 1)
    south = shifted(obj[:, :HALF, :].astype(BF16), "gy", -1)
    routed = functools.partial(
        lax.all_to_all, axis_name="gx", split_axis=0, concat_axis=0, tiled=True
    )
    first, north, south = lax.optimization_barrier((sends[0], north, south))
    amps = routed(first)

    def column(lo, hi):
        own = obj[:, :, lo:hi].astype(BF16)
        return jnp.concatenate([north[:, :, lo:hi], own, south[:, :, lo:hi]], axis=1)

    west = shifted(column(TILE - HALF, TILE), "gx", 1)
    east = shifted(column(0, HALF), "gx", -1)
    west, east, rest = lax.optimization_barrier((west, east, sends[1]))
    more = routed(rest)
    tabs = jnp.asarray(table_blocks())
    notes = amps[:, 2 * FRAME, :10].astype(jnp.int32).T
    meta = jnp.stack(
        [
            notes[5 * r] * 16 + notes[5 * r + 1] if k == 0 else
            notes[5 * r + 2] * 16 + notes[5 * r + 3] if k == 1 else notes[5 * r + 4]
            for r in range(CAP) for k in range(3)
        ]
    )
    acc, far = run_first(meta, amps, probe, tabs, obj, north, south, west, east)
    west, east, top, bottom, inner = run_last(meta, more, far, probe, tabs, acc)
    from_west = shifted(east, "gx", 1)
    from_east = shifted(west, "gx", -1)
    end = EXTENT - HALF
    to_north = across(top, from_west[:, :HALF], from_east[:, :HALF])
    to_south = across(bottom, from_west[:, end:], from_east[:, end:])
    from_north = shifted(to_south, "gy", 1)
    from_south = shifted(to_north, "gy", -1)
    steps = TILE // HALF - 1
    inner = add_pair(
        sides_kernel, inner, (2, TILE, HALF), lambda i: (0, 0, steps * i), from_west, from_east
    )
    return add_pair(
        ends_kernel, inner, (2, HALF, TILE), lambda i: (0, steps * i, 0), from_north, from_south
    )


def solution(mesh):
    placed = (
        P(None, "gy", "gx"),
        P(),
        P(("gx", "gy"), None, None),
        P(("gx", "gy"), None),
        P(("gx", "gy"), None),
    )
    return jax.shard_map(
        body, mesh=mesh, in_specs=placed, out_specs=P(None, "gy", "gx"), check_vma=False
    )
```

```python
import functools
import math

import jax
import jax.numpy as jnp
import numpy as np
from jax import lax
from jax.experimental import pallas as pl
from jax.experimental.pallas import tpu as pltpu
from jax.sharding import PartitionSpec as P

CAP = 2
FRAME = 256
HALF = 128
TILE = 512
EXTENT = TILE + 2 * HALF
PANELS = EXTENT // 128
NOTE_ROWS = 16
GROUP = 4
BF16 = jnp.bfloat16
F32 = jnp.float32


def table_blocks():
    index = np.arange(FRAME)[:, None] * np.arange(FRAME)[None, :] % FRAME
    angle = index.astype(np.float32) * np.float32(2.0 * math.pi / FRAME)
    scale = np.float32(1.0 / math.sqrt(FRAME))
    re = (np.cos(angle) * scale).astype(BF16)
    im = (-np.sin(angle) * scale).astype(BF16)
    blocks = []
    for parity in (0, 1):
        c = re[:HALF, parity::2]
        s = im[:HALF, parity::2]
        fwd_right = np.block([[c, s], [-s, c]])
        fwd_left = fwd_right.T
        inv_right = np.block([[c.T, -s.T], [s.T, c.T]])
        inv_left = inv_right.T
        blocks.append([fwd_right, fwd_left, inv_right, inv_left])
    return np.stack([blocks[p][i] for i in range(4) for p in (0, 1)]).astype(BF16)


def deinterleave():
    perm = np.zeros((FRAME, FRAME), np.float32)
    for j in range(HALF):
        perm[2 * j, j] = 1.0
        perm[2 * j + 1, HALF + j] = 1.0
    return perm.astype(BF16)


def dot(a, b):
    return jnp.dot(a, b, preferred_element_type=F32)


def prep_kernel(
    where_ref, inten_ref, perm_ref, first_ref, second_ref, stage, split, notes, ranks, sems
):
    step = pl.program_id(0)
    count = pl.num_programs(0)
    per = inten_ref.shape[0]
    groups = first_ref.shape[0]
    slot = step % 2

    def notes_copy():
        return pltpu.make_async_copy(
            notes, first_ref.at[:, pl.ds(2 * FRAME, NOTE_ROWS), :], sems.at[2 * per]
        )

    @pl.when(step == 0)
    def _():
        lane = lax.broadcasted_iota(jnp.int32, (groups, 128), 1)
        owner = lax.broadcasted_iota(jnp.int32, (groups, 128), 0)
        note = jnp.zeros((groups, 128), jnp.int32)
        for g in range(groups):
            ranks[per * count + g] = 0
        for f in range(per * count):
            mine = where_ref[f]
            rank = ranks[per * count + mine]
            ranks[f] = rank
            ranks[per * count + mine] = rank + 1
            row, col = where_ref[per * count + f], where_ref[2 * per * count + f]
            at = lane - 5 * rank
            value = jnp.where(at == 0, row // 16, jnp.where(at == 1, row % 16, 0))
            value += jnp.where(at == 2, col // 16, jnp.where(at == 3, col % 16, 0))
            value += jnp.where(at == 4, 1, 0)
            note = jnp.where(owner == mine, note + value, note)
        notes[...] = jnp.broadcast_to(note.astype(F32)[:, None, :], notes.shape).astype(BF16)
        notes_copy().start()

    for i in range(per):

        @pl.when(step >= 2)
        def _():
            pltpu.make_async_copy(
                stage.at[slot, i], second_ref.at[0], sems.at[slot * per + i]
            ).wait()

    for i in range(per):
        for h in range(2):
            split[i, h] = jnp.sqrt(inten_ref[i, :, 128 * h : 128 * h + 128])
        rows = [
            jnp.concatenate([split[i, h, pl.ds(p, HALF, 2), :] for h in range(2)], axis=1)
            for p in range(2)
        ]
        amp = jnp.concatenate(rows, axis=0).astype(BF16)
        cols = dot(amp, perm_ref[...]).astype(BF16)
        stage[slot, i, 0:FRAME, :] = cols[:, :128]
        stage[slot, i, FRAME : 2 * FRAME, :] = cols[:, 128:]
    for i in range(per):
        f = step * per + i
        mine = where_ref[f]
        rank = ranks[f]

        @pl.when(rank == 0)
        def _():
            pltpu.make_async_copy(
                stage.at[slot, i],
                first_ref.at[mine, pl.ds(0, 2 * FRAME), :],
                sems.at[slot * per + i],
            ).start()

        @pl.when(rank != 0)
        def _():
            pltpu.make_async_copy(
                stage.at[slot, i], second_ref.at[mine], sems.at[slot * per + i]
            ).start()

    @pl.when(step == count - 1)
    def _():
        notes_copy().wait()
        for s in range(2):
            for i in range(per):
                pltpu.make_async_copy(
                    stage.at[s, i], second_ref.at[0], sems.at[s * per + i]
                ).wait()


def prep(where, intensity, groups):
    frames = intensity.shape[0]
    per = 8
    return pl.pallas_call(
        prep_kernel,
        grid_spec=pltpu.PrefetchScalarGridSpec(
            num_scalar_prefetch=1,
            grid=(frames // per,),
            in_specs=[
                pl.BlockSpec((per, FRAME, FRAME), lambda s, w: (s, 0, 0)),
                pl.BlockSpec((FRAME, FRAME), lambda s, w: (0, 0)),
            ],
            out_specs=[pl.BlockSpec(memory_space=pl.ANY)] * 2,
            scratch_shapes=[
                pltpu.VMEM((2, per, 2 * FRAME, 128), BF16),
                pltpu.VMEM((per, 2, FRAME, 128), F32),
                pltpu.VMEM((groups, NOTE_ROWS, 128), BF16),
                pltpu.SMEM((frames + groups,), jnp.int32),
                pltpu.SemaphoreType.DMA((2 * per + 1,)),
            ],
        ),
        out_shape=[
            jax.ShapeDtypeStruct((groups, 2 * FRAME + NOTE_ROWS, 128), BF16),
            jax.ShapeDtypeStruct((groups, 2 * FRAME, 128), BF16),
        ],
        compiler_params=pltpu.CompilerParams(vmem_limit_bytes=56 << 20),
        cost_estimate=pl.CostEstimate(
            flops=frames * 2 * FRAME**3, bytes_accessed=frames * FRAME * FRAME * 6, transcendentals=0
        ),
        name="prep",
    )(where, intensity, jnp.asarray(deinterleave()))


def tile_copies(obj_hbm, ext_ref, sems):
    return [
        pltpu.make_async_copy(
            obj_hbm.at[part, :, pl.ds(128 * j, 128)],
            ext_ref.at[part, j + 1, pl.ds(HALF, TILE), :],
            sems.at[1 + part * (TILE // 128) + j],
        )
        for part in range(2)
        for j in range(TILE // 128)
    ]


def set_halo(north_ref, south_ref, west_ref, east_ref, ext_ref):
    for part in range(2):
        ext_ref[part, 0] = west_ref[part].astype(F32)
        ext_ref[part, PANELS - 1] = east_ref[part].astype(F32)
        for j in range(TILE // 128):
            lanes = slice(128 * j, 128 * j + 128)
            ext_ref[part, j + 1, 0:HALF, :] = north_ref[part, :, lanes].astype(F32)
            ext_ref[part, j + 1, HALF + TILE :, :] = south_ref[part, :, lanes].astype(F32)


def rows_of(m, p=0, height=FRAME):
    return slice(FRAME * m + HALF * p, FRAME * m + HALF * p + height)


def forward(places, probe_ref, table_ref, ext_ref, xs, gs, take):
    members = range(len(places))
    lane = lax.broadcasted_iota(jnp.int32, (FRAME, 128), 1)
    for m in members:
        row, col, live = places[m]
        panel = col // 128
        shift = col % 128
        back_shift = (128 - shift) % 128
        keep = lane < 128 - shift

        def cut(part):
            rolled = [
                pltpu.roll(ext_ref[part, panel + i, pl.ds(row, FRAME), :], back_shift, 1)
                for i in range(3)
            ]
            return [jnp.where(keep, rolled[i], rolled[i + 1]) for i in range(2)]

        patch_re = cut(0)
        patch_im = cut(1)
        ex_re, ex_im = [], []
        for h in range(2):
            lanes = slice(128 * h, 128 * h + 128)
            pr = probe_ref[0, :, lanes]
            pi = probe_ref[1, :, lanes]
            ex_re.append(pr * patch_re[h] - pi * patch_im[h])
            ex_im.append(pr * patch_im[h] + pi * patch_re[h])
        xs[0, rows_of(m), 0:128] = (ex_re[0] + ex_re[1]).astype(BF16)
        xs[0, rows_of(m), 128:256] = (ex_im[0] + ex_im[1]).astype(BF16)
        xs[1, rows_of(m), 0:128] = (ex_re[0] - ex_re[1]).astype(BF16)
        xs[1, rows_of(m), 128:256] = (ex_im[0] - ex_im[1]).astype(BF16)
    halves = [dot(xs[q], table_ref[q]) for q in range(2)]
    for m in members:
        for q in range(2):
            half = halves[q][rows_of(m)]
            top, bottom = half[:HALF], half[HALF:]
            lanes = slice(128 * q, 128 * q + 128)
            for p, fold in ((0, top + bottom), (1, top - bottom)):
                folded = fold.astype(BF16)
                gs[m, p, 0:HALF, lanes] = folded[:, :128]
                gs[m, p, HALF:, lanes] = folded[:, 128:]
    for m in members:
        for p in range(2):
            take(m, p, dot(table_ref[2 + p], gs[m, p]))


def update(m, p, far, amp_ref, ds):
    for q in range(2):
        lanes = slice(128 * q, 128 * q + 128)
        far_re, far_im = far[:HALF, lanes], far[HALF:, lanes]
        a = amp_ref[m, FRAME * q + HALF * p : FRAME * q + HALF * p + HALF, :].astype(F32)
        factor = a * lax.rsqrt(far_re * far_re + far_im * far_im + 1.0) - 1.0
        ds[q, rows_of(m, p, HALF), 0:128] = (far_re * factor).astype(BF16)
        ds[q, rows_of(m, p, HALF), 128:256] = (far_im * factor).astype(BF16)


def backward(places, probe_ref, table_ref, acc_ref, ds, ms):
    members = range(len(places))
    lane = lax.broadcasted_iota(jnp.int32, (HALF, 128), 1)
    evens = dot(ds[0], table_ref[4])
    odds = dot(ds[1], table_ref[5])
    for m in members:
        even, odd = evens[rows_of(m)], odds[rows_of(m)]
        for h, mid in ((0, (even + odd).astype(BF16)), (1, (even - odd).astype(BF16))):
            lanes = slice(128 * h, 128 * h + 128)
            for p in range(2):
                rows = slice(HALF * p, HALF * p + HALF)
                ms[m, p, 0:HALF, lanes] = mid[rows, :128]
                ms[m, p, HALF:, lanes] = mid[rows, 128:]
    for m in members:
        row, col, live = places[m]
        shift = col % 128
        panel = jnp.where(live > 0, col // 128, PANELS)
        even = dot(table_ref[6], ms[m, 0])
        odd = dot(table_ref[7], ms[m, 1])
        keep = lane < shift
        for v in range(2):
            back = even + odd if v == 0 else even - odd
            back_re, back_im = back[:HALF], back[HALF:]
            rows = slice(HALF * v, HALF * v + HALF)
            pr = probe_ref[0, rows]
            pi = probe_ref[1, rows]
            where = pl.ds(row + HALF * v, HALF)
            for part, term in ((0, pr * back_re + pi * back_im), (1, pr * back_im - pi * back_re)):
                left = pltpu.roll(term[:, :128], shift, 1)
                right = pltpu.roll(term[:, 128:], shift, 1)
                acc_ref[part, panel, where, :] += jnp.where(keep, 0.0, left)
                acc_ref[part, panel + 1, where, :] += jnp.where(keep, left, right)
                acc_ref[part, panel + 2, where, :] += jnp.where(keep, right, 0.0)


def places_of(meta_ref, rank, group):
    places = [[meta_ref[3 * rank + k, group * GROUP + m] for k in range(3)] for m in range(GROUP)]
    live = places[0][2]
    for place in places[1:]:
        live = live + place[2]
    return places, live > 0


def first_kernel(
    meta_ref, amp_ref, probe_ref, table_ref, north_ref, south_ref, west_ref, east_ref, obj_hbm,
    out_hbm, far_ref, ext_ref, acc_ref, sems, xs, gs, ds, ms,
):
    step = pl.program_id(0)
    groups = pl.num_programs(0) // 2

    def save():
        return pltpu.make_async_copy(acc_ref.at[:, pl.ds(0, PANELS)], out_hbm, sems.at[0])

    @pl.when(step == 0)
    def _():
        copies = tile_copies(obj_hbm, ext_ref, sems)
        for copy in copies:
            copy.start()
        acc_ref[:, 0:PANELS] = jnp.zeros_like(ext_ref)
        set_halo(north_ref, south_ref, west_ref, east_ref, ext_ref)
        for copy in copies:
            copy.wait()
        inner = slice(HALF, HALF + TILE)
        acc_ref[:, 1 : PANELS - 1, inner, :] = 2.0 * ext_ref[:, 1 : PANELS - 1, inner, :]

    places, live = places_of(meta_ref, 0, jnp.minimum(step, groups - 1))

    @pl.when(live & (step < groups))
    def _():
        def take(m, p, far):
            update(m, p, far, amp_ref, ds)

        forward(places, probe_ref, table_ref, ext_ref, xs, gs, take)
        backward(places, probe_ref, table_ref, acc_ref, ds, ms)

    @pl.when(step == groups - 1)
    def _():
        save().start()

    later, live = places_of(meta_ref, 1, jnp.maximum(step - groups, 0))

    @pl.when(live & (step >= groups))
    def _():
        def take(m, p, far):
            far_ref[m, p] = far.astype(BF16)

        forward(later, probe_ref, table_ref, ext_ref, xs, gs, take)

    @pl.when(step == pl.num_programs(0) - 1)
    def _():
        save().wait()


def last_kernel(
    meta_ref, amp_ref, far_ref, probe_ref, table_ref, start_hbm,
    near_ref, far_side_ref, top_ref, bottom_ref, inner_ref, acc_ref, start_ref, sems, ds, ms,
):
    step = pl.program_id(0)

    def load():
        return pltpu.make_async_copy(start_hbm, start_ref, sems.at[0])

    @pl.when(step == 0)
    def _():
        load().start()
        acc_ref[:, 0:PANELS] = jnp.zeros_like(start_ref)

    places, live = places_of(meta_ref, 1, step)

    @pl.when(live)
    def _():
        for m in range(GROUP):
            for p in range(2):
                update(m, p, far_ref[m, p].astype(F32), amp_ref, ds)
        backward(places, probe_ref, table_ref, acc_ref, ds, ms)

    @pl.when(step == pl.num_programs(0) - 1)
    def _():
        load().wait()

        def half_sum(part, panel, rows):
            return 0.5 * (acc_ref[part, panel, rows, :] + start_ref[part, panel, rows, :])

        for part in range(2):
            near = (PANELS - 1) * (1 - meta_ref[3 * CAP, 0])
            near_ref[part] = half_sum(part, near, slice(0, EXTENT)).astype(BF16)
            far_side_ref[part] = half_sum(part, PANELS - 1 - near, slice(0, EXTENT)).astype(BF16)
            for j in range(TILE // 128):
                lanes = slice(128 * j, 128 * j + 128)
                top_ref[part, :, lanes] = half_sum(part, j + 1, slice(0, HALF)).astype(BF16)
                inner_ref[part, :, lanes] = half_sum(part, j + 1, slice(HALF, HALF + TILE))
                rows = slice(HALF + TILE, EXTENT)
                bottom_ref[part, :, lanes] = half_sum(part, j + 1, rows).astype(BF16)


def whole(shape):
    return pl.BlockSpec(shape, lambda s, m: (0,) * len(shape))


WIDE = (2, PANELS, EXTENT, 128)
SUMS = (2, PANELS + 3, EXTENT, 128)
FLAT = (2, GROUP * FRAME, FRAME)
DEEP = (GROUP, 2, FRAME, FRAME)


def run_first(meta, amps, probe, tabs, obj, north, south, west, east):
    groups = amps.shape[0] // GROUP
    return pl.pallas_call(
        first_kernel,
        grid_spec=pltpu.PrefetchScalarGridSpec(
            num_scalar_prefetch=1,
            grid=(2 * groups,),
            in_specs=[
                pl.BlockSpec(
                    (GROUP,) + amps.shape[1:], lambda s, m: (jnp.minimum(s, groups - 1), 0, 0)
                ),
                whole((2, FRAME, FRAME)),
                whole((8, FRAME, FRAME)),
                whole(north.shape),
                whole(south.shape),
                whole(west.shape),
                whole(east.shape),
                pl.BlockSpec(memory_space=pl.ANY),
            ],
            out_specs=[
                pl.BlockSpec(memory_space=pl.ANY),
                pl.BlockSpec(DEEP, lambda s, m: (jnp.maximum(s - groups, 0), 0, 0, 0)),
            ],
            scratch_shapes=[
                pltpu.VMEM(WIDE, F32),
                pltpu.VMEM(SUMS, F32),
                pltpu.SemaphoreType.DMA((1 + 2 * TILE // 128,)),
            ]
            + [pltpu.VMEM(shape, BF16) for shape in (FLAT, DEEP, FLAT, DEEP)],
        ),
        out_shape=[
            jax.ShapeDtypeStruct(WIDE, F32),
            jax.ShapeDtypeStruct((amps.shape[0], 2, FRAME, FRAME), BF16),
        ],
        compiler_params=pltpu.CompilerParams(vmem_limit_bytes=50 << 20),
        cost_estimate=pl.CostEstimate(
            flops=2 * amps.shape[0] * 16 * FRAME**3, bytes_accessed=24 << 20, transcendentals=0
        ),
        name="first",
    )(meta, amps, probe, tabs, north, south, west, east, obj)


def run_last(meta, amps, far, probe, tabs, start):
    groups = amps.shape[0] // GROUP

    def used(s, m):
        live = m[5, s * GROUP]
        for k in range(1, GROUP):
            live = live + m[5, s * GROUP + k]
        return jnp.where(live > 0, s, 0)

    shapes = [(2, EXTENT, 128)] * 2 + [(2, HALF, TILE)] * 2 + [(2, TILE, TILE)]
    return pl.pallas_call(
        last_kernel,
        grid_spec=pltpu.PrefetchScalarGridSpec(
            num_scalar_prefetch=1,
            grid=(groups,),
            in_specs=[
                pl.BlockSpec((GROUP,) + amps.shape[1:], lambda s, m: (used(s, m), 0, 0)),
                pl.BlockSpec(DEEP, lambda s, m: (used(s, m), 0, 0, 0)),
                whole((2, FRAME, FRAME)),
                whole((8, FRAME, FRAME)),
                pl.BlockSpec(memory_space=pl.ANY),
            ],
            out_specs=[whole(shape) for shape in shapes],
            scratch_shapes=[
                pltpu.VMEM(SUMS, F32),
                pltpu.VMEM(WIDE, F32),
                pltpu.SemaphoreType.DMA((1,)),
                pltpu.VMEM(FLAT, BF16),
                pltpu.VMEM(DEEP, BF16),
            ],
        ),
        out_shape=[jax.ShapeDtypeStruct(s, d) for s, d in zip(shapes, (BF16,) * 4 + (F32,))],
        compiler_params=pltpu.CompilerParams(vmem_limit_bytes=54 << 20),
        cost_estimate=pl.CostEstimate(
            flops=amps.shape[0] * 8 * FRAME**3, bytes_accessed=20 << 20, transcendentals=0
        ),
        name="last",
    )(meta, amps, far, probe, tabs, start)


def across(base, from_west, from_east):
    left = base[:, :, :HALF].astype(F32) + from_west.astype(F32)
    right = base[:, :, TILE - HALF :].astype(F32) + from_east.astype(F32)
    return jnp.concatenate(
        [left.astype(BF16), base[:, :, HALF : TILE - HALF], right.astype(BF16)], axis=2
    )


def sides_kernel(base_ref, west_ref, east_ref, out_ref):
    inner = slice(HALF, HALF + TILE)

    @pl.when(pl.program_id(0) == 0)
    def _():
        out_ref[...] = base_ref[...] + west_ref[:, inner, :].astype(F32)

    @pl.when(pl.program_id(0) == 1)
    def _():
        out_ref[...] = base_ref[...] + east_ref[:, inner, :].astype(F32)


def ends_kernel(base_ref, north_ref, south_ref, out_ref):
    @pl.when(pl.program_id(0) == 0)
    def _():
        out_ref[...] = base_ref[...] + north_ref[...].astype(F32)

    @pl.when(pl.program_id(0) == 1)
    def _():
        out_ref[...] = base_ref[...] + south_ref[...].astype(F32)


def add_pair(kernel, base, block, place, low, high):
    strip = pl.BlockSpec(low.shape, lambda i: (0, 0, 0))
    return pl.pallas_call(
        kernel,
        grid=(2,),
        in_specs=[pl.BlockSpec(block, place), strip, strip],
        out_specs=pl.BlockSpec(block, place),
        out_shape=jax.ShapeDtypeStruct(base.shape, F32),
        input_output_aliases={0: 0},
        compiler_params=pltpu.CompilerParams(vmem_limit_bytes=50 << 20),
        name="ends",
    )(base, low, high)


def shifted(value, axis, by):
    size = lax.axis_size(axis)
    pairs = [(i, i + by) for i in range(size) if 0 <= i + by < size]
    return lax.ppermute(value, axis, pairs)


def body(obj, probe, intensity, dest, offsets):
    groups = lax.axis_size("gx")
    sends = prep(jnp.concatenate([dest.T, offsets.T]).reshape(-1), intensity, groups)
    north = shifted(obj[:, TILE - HALF :, :].astype(BF16), "gy", 1)
    south = shifted(obj[:, :HALF, :].astype(BF16), "gy", -1)
    routed = functools.partial(
        lax.all_to_all, axis_name="gx", split_axis=0, concat_axis=0, tiled=True
    )
    first, north, south = lax.optimization_barrier((sends[0], north, south))
    amps = routed(first)

    def column(lo, hi):
        own = obj[:, :, lo:hi].astype(BF16)
        return jnp.concatenate([north[:, :, lo:hi], own, south[:, :, lo:hi]], axis=1)

    west = shifted(column(TILE - HALF, TILE), "gx", 1)
    east = shifted(column(0, HALF), "gx", -1)
    west, east, rest = lax.optimization_barrier((west, east, sends[1]))
    more = routed(rest)
    tabs = jnp.asarray(table_blocks())
    notes = amps[:, 2 * FRAME, :10].astype(jnp.int32).T
    meta = jnp.stack(
        [
            notes[5 * r] * 16 + notes[5 * r + 1] if k == 0 else
            notes[5 * r + 2] * 16 + notes[5 * r + 3] if k == 1 else notes[5 * r + 4]
            for r in range(CAP) for k in range(3)
        ]
        + [jnp.full((amps.shape[0],), lax.axis_index("gx") % 2, jnp.int32)]
    )
    acc, far = run_first(meta, amps, probe, tabs, obj, north, south, west, east)
    near, far_side, top, bottom, inner = run_last(meta, more, far, probe, tabs, acc)
    groups = lax.axis_size("gx")
    apart = [(i, i + 1) for i in range(1, groups - 1, 2)]
    mates = [(i, i + 1) for i in range(0, groups - 1, 2)]
    far_side = lax.ppermute(far_side, "gx", apart + [(b, a) for a, b in apart])
    near = lax.ppermute(near, "gx", mates + [(b, a) for a, b in mates])
    odd = lax.axis_index("gx") % 2 == 1
    from_west = jnp.where(odd, near, far_side)
    from_east = jnp.where(odd, far_side, near)
    end = EXTENT - HALF
    to_north = across(top, from_west[:, :HALF], from_east[:, :HALF])
    to_south = across(bottom, from_west[:, end:], from_east[:, end:])
    from_north = shifted(to_south, "gy", 1)
    from_south = shifted(to_north, "gy", -1)
    steps = TILE // HALF - 1
    inner = add_pair(
        sides_kernel, inner, (2, TILE, HALF), lambda i: (0, 0, steps * i), from_west, from_east
    )
    return add_pair(
        ends_kernel, inner, (2, HALF, TILE), lambda i: (0, steps * i, 0), from_north, from_south
    )


def solution(mesh):
    placed = (
        P(None, "gy", "gx"),
        P(),
        P(("gx", "gy"), None, None),
        P(("gx", "gy"), None),
        P(("gx", "gy"), None),
    )
    return jax.shard_map(
        body, mesh=mesh, in_specs=placed, out_specs=P(None, "gy", "gx"), check_vma=False
    )
```
